256 devices in a mesh: depth: 4 (over x_lo, core), row: 16 (over z, x_hi), col: 4 (over y).
Axes of the slice: x: 4 (x_hi: 2, x_lo: 2; x = x_hi * 2 + x_lo), y: 4, z: 8, core: 2. Of those that a mesh axis runs over, the one named last changes fastest.
Arguments:
- alignment: bfloat16 [512, 512, 256], P('depth', ('row', 'col')), may hold values from -6 to 6
- seq_mask: int32 [512], replicated, may hold values 0 or 1
- residue_mask: int32 [512], replicated, may hold values 0 or 1
- layer_norm_gain: float32 [256], replicated, may hold values from 0.5 to 1.5
- layer_norm_bias: float32 [256], replicated, may hold values from -3 to 3
- left_projection_weight: bfloat16 [256, 32], replicated, may hold values from -0.375 to 0.375
- left_bias: float32 [32], replicated, may hold values from -3 to 3
- right_projection_weight: bfloat16 [256, 32], replicated, may hold values from -0.375 to 0.375
- right_bias: float32 [32], replicated, may hold values from -3 to 3
- out_weight: bfloat16 [1024, 128], replicated, may hold values from -0.1875 to 0.1875
- pair_grad: bfloat16 [512, 512, 128], P('row', 'col'), may hold values from -6 to 6
Outputs:
- alignment_grad: bfloat16 [512, 512, 256], P('depth', ('row', 'col'))
- left_weight_grad: float32 [256, 32], replicated
- left_bias_grad: float32 [32], replicated
- right_weight_grad: float32 [256, 32], replicated
- right_bias_grad: float32 [32], replicated
- norm_gain_grad: float32 [256], replicated
- norm_bias_grad: float32 [256], replicated
- out_weight_grad: float32 [1024, 128], replicated
The draws below stay inside these ranges and needn't reach their ends.
All inputs are finite; a program needn't handle non-finite values.
Results may differ from the reference program's by a relative error of at most 0.022.
Values may be sent and summed in bfloat16 or wider, within the bound.
A program may use at most 64 MiB of HBM per device.

```python
import math
import jax
import jax.numpy as jnp
from jax import lax

ALIGNMENT_WIDTH = 256
PROJECT_CHANNELS = 32
PAIR_W = 128
SEQUENCE_ROWS = 512
RESIDUE_TOTAL = 512


def place_ends(array, key, least, top_value):
    place = [jax.random.randint(jax.random.fold_in(key, axis), (), 0, length) for axis, length in enumerate(array.shape)]
    longest = array.shape.index(max(array.shape))
    beside = place[:longest] + [(place[longest] + 1) % array.shape[longest]] + place[longest + 1:]
    return array.at[tuple(place)].set(least).at[tuple(beside)].set(top_value)


def block_levels(stream_key, dims, shards, smallest, largest):
    loudness, own = 1.0, jax.random.fold_in(stream_key, 6)
    for dim, parts in shards:
        steps = jnp.exp(jax.random.uniform(jax.random.fold_in(own, dim), (parts,), jnp.float32, smallest / len(shards), largest / len(shards)))
        loudness = loudness * jnp.repeat(steps, dims[dim] // parts).reshape([-1 if axis == dim else 1 for axis in range(len(dims))])
    return loudness


def normal_values(rng, extent, scale, reach, cuts=(), kind=jnp.bfloat16):
    array = jax.random.normal(rng, extent, jnp.float32) * scale
    if len(cuts) > 0:
        array = block_levels(rng, extent, cuts, -0.22, 0.18) * array
    return jnp.clip(array, min=-reach, max=reach).astype(kind)


def setup_inputs(seed: int = 0) -> dict:
    seeds = jax.random.split(jax.random.key(seed), 12)
    return {
        "alignment": normal_values(seeds[0], (SEQUENCE_ROWS, RESIDUE_TOTAL, ALIGNMENT_WIDTH), 1.0, 6.0, ((0, 4), (1, 64))),
        "seq_mask": place_ends((jax.random.randint(seeds[1], (SEQUENCE_ROWS,), 0, 8) < 7).astype(jnp.int32), jax.random.fold_in(seeds[1], 1), 0, 1),
        "residue_mask": place_ends((jax.random.randint(seeds[2], (RESIDUE_TOTAL,), 0, 16) < 15).astype(jnp.int32), jax.random.fold_in(seeds[2], 1), 0, 1),
        "layer_norm_gain": jnp.clip(1.0 + 0.1 * jax.random.normal(seeds[3], (ALIGNMENT_WIDTH,), jnp.float32), 0.5, 1.5),
        "layer_norm_bias": normal_values(seeds[4], (ALIGNMENT_WIDTH,), 0.5, 3.0, (), jnp.float32),
        "left_projection_weight": normal_values(seeds[5], (ALIGNMENT_WIDTH, PROJECT_CHANNELS), ALIGNMENT_WIDTH ** -0.5, 0.375),
        "left_bias": normal_values(seeds[6], (PROJECT_CHANNELS,), 0.5, 3.0, (), jnp.float32),
        "right_projection_weight": normal_values(seeds[7], (ALIGNMENT_WIDTH, PROJECT_CHANNELS), ALIGNMENT_WIDTH ** -0.5, 0.375),
        "right_bias": normal_values(seeds[8], (PROJECT_CHANNELS,), 0.5, 3.0, (), jnp.float32),
        "out_weight": normal_values(seeds[9], (PROJECT_CHANNELS * PROJECT_CHANNELS, PAIR_W), (PROJECT_CHANNELS * PROJECT_CHANNELS) ** -0.5, 0.1875),
        "pair_grad": normal_values(seeds[10], (RESIDUE_TOTAL, RESIDUE_TOTAL, PAIR_W), 1.0, 6.0, ((0, 16), (1, 4))),
    }


def layer_norm(alignment, layer_norm_gain, layer_norm_bias):
    values = alignment.astype(jnp.float32)
    centred = values - lax.optimization_barrier(jnp.mean(values, axis=-1, keepdims=True))
    inv_std = lax.rsqrt(lax.optimization_barrier(jnp.mean(centred * centred, axis=-1, keepdims=True)) + 1e-05)
    unit_values = centred * inv_std
    normed = (unit_values * layer_norm_gain + layer_norm_bias).astype(jnp.bfloat16)
    return (unit_values, inv_std, normed)

def project(normed, weight, bias, cell_mask):
    linear = jnp.einsum('srm,mc->src', normed.astype(jnp.float32), weight.astype(jnp.float32)) + bias
    return (linear * cell_mask[:, :, None]).astype(jnp.bfloat16)

def reference(alignment, seq_mask, residue_mask, layer_norm_gain, layer_norm_bias, left_projection_weight, left_bias, right_projection_weight, right_bias, out_weight, pair_grad):
    seq_float = seq_mask.astype(jnp.float32)
    res_float = residue_mask.astype(jnp.float32)
    cell_mask = seq_float[:, None] * res_float[None, :]
    unit_values, inv_std, normed = layer_norm(alignment, layer_norm_gain, layer_norm_bias)
    left = project(normed, left_projection_weight, left_bias, cell_mask)
    right = project(normed, right_projection_weight, right_bias, cell_mask)
    seq_total, residues, chans = left.shape
    pair_width = pair_grad.shape[2]
    left_trans = jnp.transpose(left, (1, 0, 2))
    right_trans = jnp.transpose(right, (1, 0, 2))
    seq_count = jnp.sum(seq_float)
    divisor = jnp.maximum(seq_count * res_float[:, None] * res_float[None, :], 1.0)
    scaled = (pair_grad.astype(jnp.float32) / divisor[:, :, None]).astype(jnp.bfloat16)
    step_rows = math.gcd(residues, 8)

    def one_block(running, pieces):
        out_grad, right_grad = running
        left_rows, scaled_rows = pieces
        outer = jnp.einsum('isc,jsd->ijcd', left_rows.astype(jnp.float32), right_trans.astype(jnp.float32)).astype(jnp.bfloat16)
        outer_flat = outer.reshape(-1, chans * chans)
        scaled_flat = scaled_rows.reshape(-1, pair_width)
        out_grad = out_grad + jnp.dot(outer_flat.T, scaled_flat, preferred_element_type=jnp.float32)
        outer_grad = jnp.dot(scaled_flat, out_weight.T, preferred_element_type=jnp.float32).astype(jnp.bfloat16)
        outer_grad = outer_grad.reshape(step_rows, residues, chans, chans).astype(jnp.float32)
        rows_grad = jnp.einsum('ijcd,jsd->isc', outer_grad, right_trans.astype(jnp.float32))
        right_grad = right_grad + jnp.einsum('ijcd,isc->jsd', outer_grad, left_rows.astype(jnp.float32))
        return ((out_grad, right_grad), rows_grad)
    start_state = (jnp.zeros((chans * chans, pair_width), jnp.float32), jnp.zeros((residues, seq_total, chans), jnp.float32))
    blocks_in = (left_trans.reshape(residues // step_rows, step_rows, seq_total, chans), scaled.reshape(residues // step_rows, step_rows, residues, pair_width))
    (out_weight_grad, right_total), left_parts = lax.scan(one_block, start_state, blocks_in)
    left_sum = jnp.transpose(left_parts.reshape(residues, seq_total, chans), (1, 0, 2))
    right_sum = jnp.transpose(right_total, (1, 0, 2))
    left_pre_grad = (left_sum * cell_mask[:, :, None]).astype(jnp.bfloat16)
    right_pre_grad = (right_sum * cell_mask[:, :, None]).astype(jnp.bfloat16)
    normed_grad = jnp.einsum('src,mc->srm', left_pre_grad.astype(jnp.float32), left_projection_weight.astype(jnp.float32))
    normed_grad = normed_grad + jnp.einsum('src,mc->srm', right_pre_grad.astype(jnp.float32), right_projection_weight.astype(jnp.float32))
    left_weight_grad = jnp.einsum('srm,src->mc', normed.astype(jnp.float32), left_pre_grad.astype(jnp.float32))
    right_weight_grad = jnp.einsum('srm,src->mc', normed.astype(jnp.float32), right_pre_grad.astype(jnp.float32))
    left_bias_grad = lax.optimization_barrier(jnp.sum(left_pre_grad.astype(jnp.float32), axis=(0, 1)))
    right_bias_grad = lax.optimization_barrier(jnp.sum(right_pre_grad.astype(jnp.float32), axis=(0, 1)))
    norm_gain_grad = lax.optimization_barrier(jnp.sum(normed_grad * unit_values, axis=(0, 1)))
    norm_bias_grad = lax.optimization_barrier(jnp.sum(normed_grad, axis=(0, 1)))
    weighted = normed_grad * layer_norm_gain
    alignment_grad = (inv_std * (weighted - lax.optimization_barrier(jnp.mean(weighted, axis=-1, keepdims=True)) - unit_values * lax.optimization_barrier(jnp.mean(weighted * unit_values, axis=-1, keepdims=True)))).astype(jnp.bfloat16)
    return (alignment_grad, left_weight_grad, left_bias_grad, right_weight_grad, right_bias_grad, norm_gain_grad, norm_bias_grad, out_weight_grad)
```

```python
import jax
import jax.numpy as jnp
from jax import lax
from jax.experimental import pallas as pl
from jax.experimental.pallas import tpu as pltpu
from jax.sharding import PartitionSpec as P

F32, BF16 = jnp.float32, jnp.bfloat16
MESH = pl.DeviceIdType.MESH
NT = (((1,), (1,)), ((), ()))
TN = (((0,), (0,)), ((), ()))
PAIR, LEFT, RIGHT, RSUM, LSUM, W1, W2, W3, W4, W5, S1, S2, S3, S4 = range(14)


def dot(a, b):
    return jnp.dot(a, b, preferred_element_type=F32)


def dot_nt(a, b, **kw):
    return lax.dot_general(a, b, NT, preferred_element_type=F32, **kw)


def main_kernel(
    x_ref, seq_ref, res_ref, res_s, gain_ref, shift_ref, wl_ref, lb_ref, wr_ref, rb_ref, ow_ref, pair_ref,
    ag_ref, small_ref, wg_ref,
    inv1, xf, unit, norm, istd, ngrad, wt, bias, wf, wp, ps, scb, bd, og, outer, lb, lt, rf, rbuf, rt,
    rss, rsr, lss, lsr, lsf, wga, wgs, wgr, w1f, w2s, w2r, w3, w5, wgt, extra, sm, s1, s2, s3, sf,
    send_sem, recv_sem, local_sem,
):
    depth, row, col = lax.axis_index("depth"), lax.axis_index("row"), lax.axis_index("col")
    z, h = lax.div(row, 2), lax.rem(row, 2)
    q = h * 4 + col

    def zpeer(k):
        t = lax.rem(z + k, 8)
        return t, (depth, t * 2 + h, col)

    def qpeer(k):
        t = lax.rem(q + k, 8)
        return t, (depth, z * 2 + lax.div(t, 4), lax.rem(t, 4))

    def dpeer(k):
        t = lax.rem(depth + k, 4)
        return t, (t, row, col)

    def copy(which, k, src, dst, device):
        return pltpu.make_async_remote_copy(
            src_ref=src, dst_ref=dst, send_sem=send_sem.at[which, k], recv_sem=recv_sem.at[which, k],
            device_id=device, device_id_type=MESH,
        )

    def pair_copy(k):
        t, device = qpeer(k)
        return copy(PAIR, k, ps.at[t], scb.at[col, pl.ds(h * 32, 32)], device)

    def left_copy(k):
        block = lb.at[pl.ds(pl.multiple_of(q * 256, 256), 256)]
        return copy(LEFT, k, block, block, qpeer(k)[1])

    def right_copy(k):
        return copy(RIGHT, k, rbuf.at[z], rbuf.at[z], zpeer(k)[1])

    def rsum_copy(k):
        t, device = zpeer(k)
        return copy(RSUM, k, rss.at[t], rsr.at[k], device)

    def lsum_copy(k):
        t, device = qpeer(k)
        return copy(LSUM, k, lss.at[t], lsr.at[k], device)

    def w1_copy(k):
        t, device = dpeer(k)
        return copy(W1, k, wgs.at[t], wgr.at[k], device)

    def w2_copy(k):
        t, device = zpeer(k)
        return copy(W2, k, w2s.at[t], w2r.at[k], device)

    def w3_copy(k):
        return copy(W3, k, w3.at[q], w3.at[q], qpeer(k)[1])

    def w4_copy(k):
        block = w5.at[depth, pl.ds(pl.multiple_of(z * 16, 16), 16)]
        return copy(W4, k, block, block, zpeer(k)[1])

    def w5_copy(k):
        return copy(W5, k, w5.at[depth], w5.at[depth], dpeer(k)[1])

    def s1_copy(k):
        t, device = zpeer(k)
        return copy(S1, k, sm.at[t], s1.at[z], device)

    def s2_copy(k):
        return copy(S2, k, s2.at[q], s2.at[q], qpeer(k)[1])

    def s3_copy(k):
        return copy(S3, k, s3.at[depth], s3.at[depth], dpeer(k)[1])

    def s4_copy(k):
        return copy(S4, k, sf.at[z], sf.at[z], zpeer(k)[1])

    def start(make, count=8):
        for k in range(1, count):
            make(k).start()

    def arrived(make, count=8):
        for k in range(1, count):
            make(k).wait_recv()

    barrier = pltpu.get_barrier_semaphore()
    for k in range(1, 8):
        pl.semaphore_signal(barrier, inc=1, device_id=zpeer(k)[1], device_id_type=MESH)
        pl.semaphore_signal(barrier, inc=1, device_id=qpeer(k)[1], device_id_type=MESH)
    for k in range(1, 4):
        pl.semaphore_signal(barrier, inc=1, device_id=dpeer(k)[1], device_id_type=MESH)

    used = jnp.sum(seq_ref[...].astype(F32), axis=1, keepdims=True)
    res_j = res_ref[:, pl.ds(pl.multiple_of(col * 128, 128), 128)].astype(F32)
    res_j = jnp.broadcast_to(res_j, (128, 128)).T
    inv1[...] = 1.0 / jnp.maximum(used * res_j, 1.0)

    @pl.loop(0, 32)
    def _(i):
        res_i = res_s[row * 32 + i].astype(F32)
        scaled = pair_ref[i].astype(F32) * (inv1[...] * res_i + (1.0 - res_i))
        for t in range(8):
            piece = jnp.concatenate([scaled[t * 8 : t * 8 + 8], scaled[64 + t * 8 : 72 + t * 8]], axis=0)
            ps[t, i] = piece.astype(BF16)

    pl.semaphore_wait(barrier, 17)
    start(pair_copy)
    own_pair = pltpu.make_async_copy(ps.at[q], scb.at[col, pl.ds(h * 32, 32)], local_sem)
    own_pair.start()

    pick = lax.broadcasted_iota(jnp.int32, (64, 32), 0) - lax.broadcasted_iota(jnp.int32, (64, 32), 1)
    first, second = (pick == 0).astype(F32), (pick == 32).astype(F32)
    wt[...] = (dot_nt(first.astype(BF16), wl_ref[...]) + dot_nt(second.astype(BF16), wr_ref[...])).astype(BF16)
    exact = dict(precision=lax.Precision.HIGHEST)
    bias[...] = dot_nt(first, jnp.broadcast_to(lb_ref[...], (128, 32)), **exact) + dot_nt(
        second, jnp.broadcast_to(rb_ref[...], (128, 32)), **exact
    )
    for e in range(2):
        xf[e] = x_ref[:, e * 128 : e * 128 + 128].astype(F32)
    seq_row = seq_ref[:, pl.ds(pl.multiple_of(depth * 128, 128), 128)].astype(F32)
    own_first = (row * 4 + col) * 8

    @pl.loop(0, 8)
    def _(r):
        values = jnp.concatenate([xf[e, pl.ds(r, 128, stride=8), :] for e in range(2)], axis=1)
        centred = values - jnp.mean(values, axis=1, keepdims=True)
        inv_std = lax.rsqrt(jnp.mean(centred * centred, axis=1, keepdims=True) + 1e-05)
        units = centred * inv_std
        normed = (units * gain_ref[...] + shift_ref[...]).astype(BF16)
        unit[r] = units
        norm[r] = normed
        istd[r] = jnp.broadcast_to(inv_std, (128, 128))
        mask = seq_row * res_s[own_first + r].astype(F32)
        both = (dot_nt(wt[...], normed) + bias[...]) * mask
        lb[pl.ds(pl.multiple_of(q * 256 + r * 32, 32), 32), :] = both[:32].astype(BF16)
        rf[pl.ds(r, 32, stride=8), :] = both[32:]

    rbuf[z] = rf[...].astype(BF16)
    start(left_copy)
    start(right_copy)

    wf[...] = ow_ref[...].astype(F32)
    for d in range(32):
        wp[d // 2 * 32 : d // 2 * 32 + 32, d % 2 * 128 : d % 2 * 128 + 128] = wf[pl.ds(d, 32, stride=32), :].astype(BF16)

    @pl.loop(0, 64)
    def _(i):
        bd[i] = jnp.zeros((128, 256), BF16)

    own_pair.wait()
    arrived(pair_copy)

    @pl.loop(0, 32)
    def _(t):
        for e in range(2):
            block = jnp.concatenate([scb[y, 2 * t + e] for y in range(4)], axis=0)
            bd[2 * t + e, :64, :128] = block
            bd[2 * t + e, 64:, 128:] = block
        grads = dot_nt(wp[...], bd[pl.ds(2 * t, 2)].reshape(256, 256)).astype(BF16)
        for e in range(2):
            at = pl.ds(pl.multiple_of((2 * t + e) * 32, 32), 32)
            for p in range(16):
                og[at, p * 128 : p * 128 + 128] = grads[p * 32 : p * 32 + 32, e * 128 : e * 128 + 128]

    arrived(left_copy)
    for t in range(16):
        block = lb[t * 128 : t * 128 + 128, :].astype(F32)
        lt[:, t * 128 : t * 128 + 128] = block.T.astype(BF16)

    @pl.loop(0, 8)
    def _(n):
        sums = dot(lt[...], og[:, pl.ds(pl.multiple_of(n * 256, 256), 256)])
        for e in range(2):
            turned = sums[:, e * 128 : e * 128 + 128].T
            for t in range(8):
                piece = jnp.concatenate([turned[t * 8 : t * 8 + 8], turned[64 + t * 8 : 72 + t * 8]], axis=0)
                rss[t, pl.ds(pl.multiple_of((2 * n + e) * 16, 16), 16), :] = piece.astype(BF16)

    start(rsum_copy)

    arrived(right_copy)

    @pl.loop(0, 16)
    def _(p):
        blocks = [rbuf[t, pl.ds(pl.multiple_of(p * 16, 16), 16), :].astype(F32) for t in range(8)]
        rows = [block[:8] for block in blocks] + [block[8:] for block in blocks]
        rt[pl.ds(pl.multiple_of(p * 128, 128), 128), :] = jnp.concatenate(rows, axis=0).astype(BF16)

    def left_sum(t):
        at = pl.ds(pl.multiple_of(t * 256, 256), 256)
        lss[t] = dot(og[at, :], rt[...]).astype(BF16)

    @pl.loop(1, 8)
    def _(k):
        left_sum(lax.rem(q + k, 8))
        lsum_copy(k).start()

    left_sum(q)

    @pl.loop(0, 8)
    def _(n):
        at = pl.ds(pl.multiple_of(n * 256, 256), 256)
        for m in range(4):
            product = dot_nt(lb[m * 512 : m * 512 + 512, :], rt[at, :])
            outer[m * 512 : m * 512 + 512, at] = product.astype(BF16)

    wga[...] = jnp.zeros_like(wga)

    @pl.loop(0, 16)
    def _(t):
        blocks = [outer[pl.ds(pl.multiple_of((4 * t + e) * 32, 32), 32), :] for e in range(4)]
        rows = [
            jnp.concatenate([block[:, p * 128 : p * 128 + 128] for block in blocks], axis=1) for p in range(16)
        ]
        wga[...] += dot(jnp.concatenate(rows, axis=0), bd[pl.ds(4 * t, 4)].reshape(512, 256))

    for t in range(4):
        wgs[t] = wga[t * 128 : t * 128 + 128, :].astype(BF16)
    start(w1_copy, 4)

    arrived(lsum_copy)
    total = lss[q].astype(F32)
    for k in range(1, 8):
        total = total + lsr[k].astype(F32)
    lsf[...] = total
    arrived(rsum_copy)
    total = rss[z].astype(F32)
    for k in range(1, 8):
        total = total + rsr[k].astype(F32)
    rf[...] = total

    wgt[...] = jnp.zeros_like(wgt)
    extra[...] = jnp.zeros_like(extra)

    @pl.loop(0, 8)
    def _(r):
        mask = seq_row * res_s[own_first + r].astype(F32)
        sides = [lsf[pl.ds(pl.multiple_of(r * 32, 32), 32), :], rf[pl.ds(r, 32, stride=8), :]]
        pre = (jnp.concatenate(sides, axis=0) * mask).astype(BF16)
        grad = lax.dot_general(pre, wt[...], TN, preferred_element_type=F32)
        ngrad[r] = grad
        wgt[...] += dot(pre, norm[r])
        extra[0:1, :] += jnp.sum(grad * unit[r], axis=0, keepdims=True)
        extra[1:2, :] += jnp.sum(grad, axis=0, keepdims=True)
        extra[2:3, 0:64] += dot_nt(jnp.ones((8, 128), BF16), pre)[0:1]

    for t in range(8):
        sm[t, 0:8] = wgt[t * 8 : t * 8 + 8, :]
        sm[t, 8:16] = extra[...]
    s1[z] = sm[z]
    start(s1_copy)

    def input_grad(r):
        units = unit[r]
        weighted = ngrad[r] * gain_ref[...]
        mean = jnp.mean(weighted, axis=1, keepdims=True)
        along = jnp.mean(weighted * units, axis=1, keepdims=True)
        scale = jnp.concatenate([istd[r], istd[r]], axis=1)
        result = scale * (weighted - mean - units * along)
        for e in range(2):
            xf[e, pl.ds(r, 128, stride=8), :] = result[:, e * 128 : e * 128 + 128]

    def summed(ref, count):
        total = ref[0]
        for k in range(1, count):
            total = total + ref[k]
        return total

    arrived(w1_copy, 4)
    total = wga[pl.ds(pl.multiple_of(depth * 128, 128), 128), :]
    for k in range(1, 4):
        total = total + wgr[k].astype(F32)
    w1f[...] = total
    for t in range(8):
        w2s[t] = w1f[t * 16 : t * 16 + 16, :].astype(BF16)
    start(w2_copy)

    @pl.loop(0, 3)
    def _(r):
        input_grad(r)

    arrived(s1_copy)
    s2[q] = summed(s1, 8)
    start(s2_copy)

    arrived(w2_copy)
    total = w1f[pl.ds(pl.multiple_of(z * 16, 16), 16), :]
    for k in range(1, 8):
        total = total + w2r[k].astype(F32)
    w3[q] = total
    start(w3_copy)

    @pl.loop(3, 6)
    def _(r):
        input_grad(r)

    arrived(s2_copy)
    s3[depth] = summed(s2, 8)
    start(s3_copy, 4)

    arrived(w3_copy)
    w5[depth, pl.ds(pl.multiple_of(z * 16, 16), 16), :] = summed(w3, 8).astype(BF16)
    start(w4_copy)

    @pl.loop(6, 8)
    def _(r):
        input_grad(r)

    arrived(s3_copy, 4)
    total = summed(s3, 4)
    sf[z] = total[:8]
    start(s4_copy)
    small_ref[64:72, :] = total[8:]

    arrived(w4_copy)
    start(w5_copy, 4)

    for e in range(2):
        ag_ref[:, e * 128 : e * 128 + 128] = xf[e].astype(BF16)

    arrived(s4_copy)
    for t in range(8):
        small_ref[t * 8 : t * 8 + 8, :] = sf[t]
    arrived(w5_copy, 4)
    for t in range(4):
        wg_ref[t * 128 : t * 128 + 128, :] = w5[t]

    for make in (pair_copy, left_copy, right_copy, rsum_copy, lsum_copy, w2_copy, w3_copy, w4_copy, s1_copy, s2_copy,
                 s4_copy):
        for k in range(1, 8):
            make(k).wait_send()
    for make in (w1_copy, w5_copy, s3_copy):
        for k in range(1, 4):
            make(k).wait_send()


def last_kernel(ag_in, small, wg, ag_ref, lw_ref, lb_ref, rw_ref, rb_ref, gain_ref, shift_ref, ow_ref):
    ag_ref[...] = ag_in[...]
    turned = small[0:64, :].T
    lw_ref[...] = turned[:, :32]
    rw_ref[...] = turned[:, 32:]
    gain_ref[...] = small[64:65, :]
    shift_ref[...] = small[65:66, :]
    lb_ref[...] = small[66:67, 0:32]
    rb_ref[...] = small[66:67, 32:64]
    for d in range(32):
        tile = wg[d // 2 * 32 : d // 2 * 32 + 32, d % 2 * 128 : d % 2 * 128 + 128]
        ow_ref[pl.ds(d, 32, stride=32), :] = tile.astype(F32)


def body(
    alignment, seq_mask, residue_mask, layer_norm_gain, layer_norm_bias, left_projection_weight, left_bias,
    right_projection_weight, right_bias, out_weight, pair_grad,
):
    vmem = pl.BlockSpec(memory_space=pltpu.VMEM)
    smem = pl.BlockSpec(memory_space=pltpu.SMEM)
    v = pltpu.VMEM
    shape = jax.ShapeDtypeStruct
    scratch = [
        v((128, 128), F32),
        v((2, 1024, 128), F32),
        v((8, 128, 256), F32),
        v((8, 128, 256), BF16),
        v((8, 128, 128), F32),
        v((8, 128, 256), F32),
        v((64, 256), BF16),
        v((64, 128), F32),
        v((1024, 128), F32),
        v((512, 256), BF16),
        v((8, 32, 16, 128), BF16),
        v((4, 64, 16, 128), BF16),
        v((64, 128, 256), BF16),
        v((2048, 2048), BF16),
        v((2048, 2048), BF16),
        v((2048, 128), BF16),
        v((128, 2048), BF16),
        v((256, 128), F32),
        v((8, 256, 128), BF16),
        v((2048, 128), BF16),
        v((8, 256, 128), BF16),
        v((8, 256, 128), BF16),
        v((8, 256, 128), BF16),
        v((8, 256, 128), BF16),
        v((256, 128), F32),
        v((512, 256), F32),
        v((4, 128, 256), BF16),
        v((4, 128, 256), BF16),
        v((128, 256), F32),
        v((8, 16, 256), BF16),
        v((8, 16, 256), BF16),
        v((8, 16, 256), F32),
        v((4, 128, 256), BF16),
        v((64, 256), F32),
        v((8, 256), F32),
        v((8, 16, 256), F32),
        v((8, 16, 256), F32),
        v((8, 16, 256), F32),
        v((4, 16, 256), F32),
        v((8, 8, 256), F32),
        pltpu.SemaphoreType.DMA((14, 8)),
        pltpu.SemaphoreType.DMA((14, 8)),
        pltpu.SemaphoreType.DMA,
    ]
    ag, small, wg = pl.pallas_call(
        main_kernel,
        out_shape=(shape((1024, 256), BF16), shape((72, 256), F32), shape((512, 256), BF16)),
        in_specs=[vmem] * 3 + [smem] + [vmem] * 8,
        out_specs=(vmem,) * 3,
        scratch_shapes=scratch,
        compiler_params=pltpu.CompilerParams(
            collective_id=0, has_side_effects=True, vmem_limit_bytes=58 * 1024 * 1024
        ),
        name="pair_backward",
    )(
        alignment.reshape(1024, 256), seq_mask.reshape(1, 512), residue_mask.reshape(1, 512), residue_mask,
        layer_norm_gain.reshape(1, 256), layer_norm_bias.reshape(1, 256), left_projection_weight,
        left_bias.reshape(1, 32), right_projection_weight, right_bias.reshape(1, 32), out_weight, pair_grad,
    )
    ag, lw, lbg, rw, rbg, gain, shift, ow = pl.pallas_call(
        last_kernel,
        out_shape=(
            shape((1024, 256), BF16), shape((256, 32), F32), shape((1, 32), F32), shape((256, 32), F32),
            shape((1, 32), F32), shape((1, 256), F32), shape((1, 256), F32), shape((1024, 128), F32),
        ),
        in_specs=[vmem] * 3,
        out_specs=(vmem,) * 8,
        compiler_params=pltpu.CompilerParams(vmem_limit_bytes=32 * 1024 * 1024),
        name="lay_out",
    )(ag, small, wg)
    return (
        ag.reshape(128, 8, 256), lw, lbg.reshape(32), rw, rbg.reshape(32), gain.reshape(256), shift.reshape(256), ow,
    )


def solution(mesh):
    placed = (P("depth", ("row", "col"), None),) + (P(),) * 9 + (P("row", "col", None),)
    return jax.shard_map(
        body,
        mesh=mesh,
        in_specs=placed,
        out_specs=(P("depth", ("row", "col"), None),) + (P(),) * 7,
        check_vma=False,
    )
```

```python
import jax
import jax.numpy as jnp
from jax import lax
from jax.experimental import pallas as pl
from jax.experimental.pallas import tpu as pltpu
from jax.sharding import PartitionSpec as P

F32, BF16 = jnp.float32, jnp.bfloat16
MESH = pl.DeviceIdType.MESH
NT = (((1,), (1,)), ((), ()))
TN = (((0,), (0,)), ((), ()))
PAIR, LEFT, RIGHT, RSUM, RSUM2, LSUM = range(6)
W1, W2, W3, S1, S2, S3 = range(6)


def dot(a, b):
    return jnp.dot(a, b, preferred_element_type=F32)


def dot_nt(a, b, **kw):
    return lax.dot_general(a, b, NT, preferred_element_type=F32, **kw)


def main_kernel(
    x_ref, seq_ref, res_ref, res_s, gain_ref, shift_ref, wl_ref, lb_ref, wr_ref, rb_ref, ow_ref, pair_ref,
    ag_ref, sf_ref, wg_ref,
    inv1, xf, unit, norm, istd, ngrad, wt, bias, wf, wp, ps, scb, bd, og, outer, lb, lt, rf, rbuf, rt,
    rss, rsr, lss, lsr, lsf, wga, w1s, w1r, w2, w3, wgt, extra, s1s, s1r, s2, s3,
    send_sem, recv_sem, group_send, group_recv, local_sem,
):
    depth, row, col = lax.axis_index("depth"), lax.axis_index("row"), lax.axis_index("col")
    z, h = lax.div(row, 2), lax.rem(row, 2)
    q = h * 4 + col

    def zpeer(k):
        t = lax.rem(z + k, 8)
        return t, (depth, t * 2 + h, col)

    def qpeer(k):
        t = lax.rem(q + k, 8)
        return t, (depth, z * 2 + lax.div(t, 4), lax.rem(t, 4))

    g = depth * 8 + q

    def gpeer(k):
        t = lax.rem(g + k, 32)
        u = lax.rem(t, 8)
        return t, (lax.div(t, 8), z * 2 + lax.div(u, 4), lax.rem(u, 4))

    def copy(which, k, src, dst, device):
        return pltpu.make_async_remote_copy(
            src_ref=src, dst_ref=dst, send_sem=send_sem.at[which, k], recv_sem=recv_sem.at[which, k],
            device_id=device, device_id_type=MESH,
        )

    def pair_copy(k):
        t, device = qpeer(k)
        return copy(PAIR, k, ps.at[t], scb.at[col, pl.ds(h * 32, 32)], device)

    def left_copy(k):
        block = lb.at[pl.ds(pl.multiple_of(q * 256, 256), 256)]
        return copy(LEFT, k, block, block, qpeer(k)[1])

    def right_copy(k):
        return copy(RIGHT, k, rbuf.at[z], rbuf.at[z], zpeer(k)[1])

    def rsum_copy(k, part=0):
        t, device = zpeer(k)
        half = pl.ds(part * 128, 128)
        return copy(RSUM + part, k, rss.at[t, half], rsr.at[k, half], device)

    def rsum2_copy(k):
        return rsum_copy(k, 1)

    def lsum_copy(k):
        t, device = qpeer(k)
        return copy(LSUM, k, lss.at[t], lsr.at[k], device)

    def group_copy(which, src, dst, device):
        return pltpu.make_async_remote_copy(
            src_ref=src, dst_ref=dst, send_sem=group_send.at[which], recv_sem=group_recv.at[which],
            device_id=device, device_id_type=MESH,
        )

    def scatter_plane(which, src, dst):
        @pl.loop(1, 32)
        def _(k):
            t, device = gpeer(k)
            group_copy(which, src.at[t], dst.at[k], device).start()

    def share_line(which, ref):
        for k in range(1, 8):
            group_copy(which, ref.at[z], ref.at[z], zpeer(k)[1]).start()

    def gather_plane(which, ref):
        @pl.loop(1, 32)
        def _(k):
            group_copy(which, ref.at[g], ref.at[g], gpeer(k)[1]).start()

    def group_wait(which, ref, sems):
        count = ref.shape[0] - 1
        pltpu.make_async_copy(ref.at[pl.ds(1, count)], ref.at[pl.ds(1, count)], sems.at[which]).wait()

    def start(make, count=8):
        for k in range(1, count):
            make(k).start()

    def arrived(make, count=8):
        for k in range(1, count):
            make(k).wait_recv()

    barrier = pltpu.get_barrier_semaphore()
    for k in range(1, 8):
        pl.semaphore_signal(barrier, inc=1, device_id=zpeer(k)[1], device_id_type=MESH)

    @pl.loop(1, 32)
    def _(k):
        pl.semaphore_signal(barrier, inc=1, device_id=gpeer(k)[1], device_id_type=MESH)

    used = jnp.sum(seq_ref[...].astype(F32), axis=1, keepdims=True)
    res_j = res_ref[:, pl.ds(pl.multiple_of(col * 128, 128), 128)].astype(F32)
    res_j = jnp.broadcast_to(res_j, (128, 128)).T
    inv1[...] = 1.0 / jnp.maximum(used * res_j, 1.0)

    @pl.loop(0, 32)
    def _(i):
        res_i = res_s[row * 32 + i].astype(F32)
        scaled = pair_ref[i].astype(F32) * (inv1[...] * res_i + (1.0 - res_i))
        for t in range(8):
            piece = jnp.concatenate([scaled[t * 8 : t * 8 + 8], scaled[64 + t * 8 : 72 + t * 8]], axis=0)
            ps[t, i] = piece.astype(BF16)

    pl.semaphore_wait(barrier, 38)
    start(pair_copy)
    own_pair = pltpu.make_async_copy(ps.at[q], scb.at[col, pl.ds(h * 32, 32)], local_sem)
    own_pair.start()

    pick = lax.broadcasted_iota(jnp.int32, (64, 32), 0) - lax.broadcasted_iota(jnp.int32, (64, 32), 1)
    first, second = (pick == 0).astype(F32), (pick == 32).astype(F32)
    wt[0:32, :] = wl_ref[...]
    wt[32:64, :] = wr_ref[...]
    exact = dict(precision=lax.Precision.HIGHEST)
    bias[...] = dot_nt(first, jnp.broadcast_to(lb_ref[...], (128, 32)), **exact) + dot_nt(
        second, jnp.broadcast_to(rb_ref[...], (128, 32)), **exact
    )
    for e in range(2):
        xf[e] = x_ref[:, e * 128 : e * 128 + 128].astype(F32)
    seq_row = seq_ref[:, pl.ds(pl.multiple_of(depth * 128, 128), 128)].astype(F32)
    own_first = (row * 4 + col) * 8

    @pl.loop(0, 8, unroll=4)
    def _(r):
        values = jnp.concatenate([xf[e, pl.ds(r, 128, stride=8), :] for e in range(2)], axis=1)
        centred = values - jnp.mean(values, axis=1, keepdims=True)
        inv_std = lax.rsqrt(jnp.mean(centred * centred, axis=1, keepdims=True) + 1e-05)
        units = centred * inv_std
        normed = (units * gain_ref[...] + shift_ref[...]).astype(BF16)
        unit[r] = units
        norm[r] = normed
        istd[r] = jnp.broadcast_to(inv_std, (128, 128))
        mask = seq_row * res_s[own_first + r].astype(F32)
        both = (dot_nt(wt[...], normed) + bias[...]) * mask
        lb[pl.ds(pl.multiple_of(q * 256 + r * 32, 32), 32), :] = both[:32].astype(BF16)
        rf[pl.ds(r, 32, stride=8), :] = both[32:]

    rbuf[z] = rf[...].astype(BF16)
    start(left_copy)
    start(right_copy)

    wf[...] = ow_ref[...].astype(F32)
    for d in range(32):
        wp[d // 2 * 32 : d // 2 * 32 + 32, d % 2 * 128 : d % 2 * 128 + 128] = wf[pl.ds(d, 32, stride=32), :].astype(BF16)

    @pl.loop(0, 64)
    def _(i):
        bd[i] = jnp.zeros((128, 256), BF16)

    own_pair.wait()
    arrived(pair_copy)

    @pl.loop(0, 32, unroll=8)
    def _(t):
        for e in range(2):
            block = jnp.concatenate([scb[y, 2 * t + e] for y in range(4)], axis=0)
            bd[2 * t + e, :64, :128] = block
            bd[2 * t + e, 64:, 128:] = block
        grads = dot_nt(wp[...], bd[pl.ds(2 * t, 2)].reshape(256, 256)).astype(BF16)
        for e in range(2):
            at = pl.ds(pl.multiple_of((2 * t + e) * 32, 32), 32)
            for p in range(16):
                og[at, p * 128 : p * 128 + 128] = grads[p * 32 : p * 32 + 32, e * 128 : e * 128 + 128]

    arrived(left_copy)
    for t in range(16):
        block = lb[t * 128 : t * 128 + 128, :].astype(F32)
        lt[:, t * 128 : t * 128 + 128] = block.T.astype(BF16)

    def right_sums(part):
        sums = dot(lt[...], og[:, part * 1024 : part * 1024 + 1024])
        for p in range(8):
            turned = sums[:, p * 128 : p * 128 + 128].T
            at = part * 128 + p * 16
            for t in range(8):
                piece = jnp.concatenate([turned[t * 8 : t * 8 + 8], turned[64 + t * 8 : 72 + t * 8]], axis=0)
                rss[t, at : at + 16, :] = piece.astype(BF16)

    right_sums(0)
    start(rsum_copy)
    right_sums(1)
    start(rsum2_copy)

    arrived(right_copy)

    @pl.loop(0, 16)
    def _(p):
        blocks = [rbuf[t, pl.ds(pl.multiple_of(p * 16, 16), 16), :].astype(F32) for t in range(8)]
        rows = [block[:8] for block in blocks] + [block[8:] for block in blocks]
        rt[pl.ds(pl.multiple_of(p * 128, 128), 128), :] = jnp.concatenate(rows, axis=0).astype(BF16)

    def left_sum(t):
        at = pl.ds(pl.multiple_of(t * 256, 256), 256)
        lss[t] = dot(og[at, :], rt[...]).astype(BF16)

    @pl.loop(1, 8)
    def _(k):
        left_sum(lax.rem(q + k, 8))
        lsum_copy(k).start()

    left_sum(q)

    @pl.loop(0, 8, unroll=4)
    def _(n):
        at = pl.ds(pl.multiple_of(n * 256, 256), 256)
        for m in range(4):
            product = dot_nt(lb[m * 512 : m * 512 + 512, :], rt[at, :])
            outer[m * 512 : m * 512 + 512, at] = product.astype(BF16)

    wga[...] = jnp.zeros_like(wga)

    @pl.loop(0, 4)
    def _(t):
        blocks = [outer[pl.ds(pl.multiple_of((16 * t + e) * 32, 32), 32), :] for e in range(16)]
        rows = [
            jnp.concatenate([block[:, p * 128 : p * 128 + 128] for block in blocks], axis=1) for p in range(16)
        ]
        wga[...] += dot(jnp.concatenate(rows, axis=0), bd[pl.ds(16 * t, 16)].reshape(2048, 256))

    for t in range(32):
        w1s[t] = wga[t * 16 : t * 16 + 16, :].astype(BF16)
    scatter_plane(W1, w1s, w1r)

    arrived(lsum_copy)
    total = lss[q].astype(F32)
    for k in range(1, 8):
        total = total + lsr[k].astype(F32)
    lsf[...] = total
    arrived(rsum_copy)
    arrived(rsum2_copy)
    total = rss[z].astype(F32)
    for k in range(1, 8):
        total = total + rsr[k].astype(F32)
    rf[...] = total

    wgt[...] = jnp.zeros_like(wgt)
    extra[...] = jnp.zeros_like(extra)

    @pl.loop(0, 8, unroll=4)
    def _(r):
        mask = seq_row * res_s[own_first + r].astype(F32)
        sides = [lsf[pl.ds(pl.multiple_of(r * 32, 32), 32), :], rf[pl.ds(r, 32, stride=8), :]]
        pre = (jnp.concatenate(sides, axis=0) * mask).astype(BF16)
        grad = lax.dot_general(pre, wt[...], TN, preferred_element_type=F32)
        ngrad[r] = grad
        wgt[...] += dot(pre, norm[r])
        extra[0:1, :] += jnp.sum(grad * unit[r], axis=0, keepdims=True)
        extra[1:2, :] += jnp.sum(grad, axis=0, keepdims=True)
        extra[2:3, 0:64] += dot_nt(jnp.ones((8, 128), BF16), pre)[0:1]

    upper = lax.broadcasted_iota(jnp.int32, (8, 128), 0) < 4
    for t in range(16):
        tile = wgt[t // 2 * 8 : t // 2 * 8 + 8, t % 2 * 128 : t % 2 * 128 + 128]
        s1s[2 * t] = jnp.where(upper, tile, 0.0)
        s1s[2 * t + 1] = jnp.where(upper, 0.0, tile)
    s1s[0, 4:5, :] = extra[0:1, :128]
    s1s[1, 0:1, :] = extra[0:1, 128:]
    s1s[2, 4:5, :] = extra[1:2, :128]
    s1s[3, 0:1, :] = extra[1:2, 128:]
    s1s[4, 4:5, :] = extra[2:3, :128]
    scatter_plane(S1, s1s, s1r)

    def input_grad(r):
        units = unit[r]
        weighted = ngrad[r] * gain_ref[...]
        mean = jnp.mean(weighted, axis=1, keepdims=True)
        along = jnp.mean(weighted * units, axis=1, keepdims=True)
        scale = jnp.concatenate([istd[r], istd[r]], axis=1)
        result = scale * (weighted - mean - units * along)
        for e in range(2):
            xf[e, pl.ds(r, 128, stride=8), :] = result[:, e * 128 : e * 128 + 128]

    def summed(ref, count, first):
        total = first
        for k in range(1, count):
            total = total + ref[k].astype(F32)
        return total

    @pl.loop(0, 4, unroll=4)
    def _(r):
        input_grad(r)

    group_wait(W1, w1r, group_recv)
    w2[z] = summed(w1r, 32, wga[pl.ds(pl.multiple_of(g * 16, 16), 16), :]).astype(BF16)
    share_line(W2, w2)
    group_wait(S1, s1r, group_recv)
    s2[z] = summed(s1r, 32, s1s[g])
    share_line(S2, s2)

    @pl.loop(4, 8, unroll=4)
    def _(r):
        input_grad(r)

    for e in range(2):
        ag_ref[:, e * 128 : e * 128 + 128] = xf[e].astype(BF16)

    group_wait(W2, w2, group_recv)
    w3[g] = summed(w2, 8, w2[0].astype(F32)).astype(BF16)
    gather_plane(W3, w3)
    group_wait(S2, s2, group_recv)
    s3[g] = summed(s2, 8, s2[0])
    gather_plane(S3, s3)

    for make in (pair_copy, left_copy, right_copy, rsum_copy, rsum2_copy, lsum_copy):
        for k in range(1, 8):
            make(k).wait_send()
    for which, ref in ((W1, w1s), (W2, w2), (W3, w3), (S1, s1s), (S2, s2), (S3, s3)):
        group_wait(which, ref, group_send)

    group_wait(W3, w3, group_recv)
    for t in range(32):
        wg_ref[t * 16 : t * 16 + 16, :] = w3[t]
    group_wait(S3, s3, group_recv)
    sf_ref[...] = s3[...]


def last_kernel(
    ag_any, sf_any, wg_any, ag_out, lw_ref, lb_ref, rw_ref, rb_ref, gain_ref, shift_ref, ow_ref, sf, wg, sems
):
    moves = [
        pltpu.make_async_copy(src, dst, sems.at[n])
        for n, (src, dst) in enumerate(((wg_any, wg), (sf_any, sf), (ag_any, ag_out)))
    ]
    for move in moves:
        move.start()
    moves[0].wait()
    for d in range(32):
        tile = wg[d // 2 * 32 : d // 2 * 32 + 32, d % 2 * 128 : d % 2 * 128 + 128]
        ow_ref[pl.ds(d, 32, stride=32), :] = tile.astype(F32)
    moves[1].wait()
    upper = lax.broadcasted_iota(jnp.int32, (8, 128), 0) < 4
    for t in range(16):
        tile = jnp.where(upper, sf[2 * t], sf[2 * t + 1])
        side, row, lane = (lw_ref, rw_ref)[t // 8], t % 8 // 2 * 8, t % 2 * 128
        side[row : row + 8, lane : lane + 128] = tile
    gain_ref[:, :128] = sf[0, 4:5, :]
    gain_ref[:, 128:] = sf[1, 0:1, :]
    shift_ref[:, :128] = sf[2, 4:5, :]
    shift_ref[:, 128:] = sf[3, 0:1, :]
    lb_ref[...] = sf[4, 4:5, 0:32]
    rb_ref[...] = sf[4, 4:5, 32:64]
    moves[2].wait()


def body(
    alignment, seq_mask, residue_mask, layer_norm_gain, layer_norm_bias, left_projection_weight, left_bias,
    right_projection_weight, right_bias, out_weight, pair_grad,
):
    vmem = pl.BlockSpec(memory_space=pltpu.VMEM)
    smem = pl.BlockSpec(memory_space=pltpu.SMEM)
    v = pltpu.VMEM
    shape = jax.ShapeDtypeStruct
    scratch = [
        v((128, 128), F32),
        v((2, 1024, 128), F32),
        v((8, 128, 256), F32),
        v((8, 128, 256), BF16),
        v((8, 128, 128), F32),
        v((8, 128, 256), F32),
        v((64, 256), BF16),
        v((64, 128), F32),
        v((1024, 128), F32),
        v((512, 256), BF16),
        v((8, 32, 16, 128), BF16),
        v((4, 64, 16, 128), BF16),
        v((64, 128, 256), BF16),
        v((2048, 2048), BF16),
        v((2048, 2048), BF16),
        v((2048, 128), BF16),
        v((128, 2048), BF16),
        v((256, 128), F32),
        v((8, 256, 128), BF16),
        v((2048, 128), BF16),
        v((8, 256, 128), BF16),
        v((8, 256, 128), BF16),
        v((8, 256, 128), BF16),
        v((8, 256, 128), BF16),
        v((256, 128), F32),
        v((512, 256), F32),
        v((32, 16, 256), BF16),
        v((32, 16, 256), BF16),
        v((8, 16, 256), BF16),
        v((32, 16, 256), BF16),
        v((64, 256), F32),
        v((8, 256), F32),
        v((32, 8, 128), F32),
        v((32, 8, 128), F32),
        v((8, 8, 128), F32),
        v((32, 8, 128), F32),
        pltpu.SemaphoreType.DMA((6, 8)),
        pltpu.SemaphoreType.DMA((6, 8)),
        pltpu.SemaphoreType.DMA((6,)),
        pltpu.SemaphoreType.DMA((6,)),
        pltpu.SemaphoreType.DMA,
    ]
    ag, sf, wg = pl.pallas_call(
        main_kernel,
        out_shape=(shape((1024, 256), BF16), shape((32, 8, 128), F32), shape((512, 256), BF16)),
        in_specs=[vmem] * 3 + [smem] + [vmem] * 8,
        out_specs=(vmem,) * 3,
        scratch_shapes=scratch,
        compiler_params=pltpu.CompilerParams(
            collective_id=0, has_side_effects=True, vmem_limit_bytes=58 * 1024 * 1024
        ),
        name="pair_backward",
    )(
        alignment.reshape(1024, 256), seq_mask.reshape(1, 512), residue_mask.reshape(1, 512), residue_mask,
        layer_norm_gain.reshape(1, 256), layer_norm_bias.reshape(1, 256), left_projection_weight.T,
        left_bias.reshape(1, 32), right_projection_weight.T, right_bias.reshape(1, 32), out_weight, pair_grad,
    )
    ag, lw, lbg, rw, rbg, gain, shift, ow = pl.pallas_call(
        last_kernel,
        out_shape=(
            shape((1024, 256), BF16), shape((32, 256), F32), shape((1, 32), F32), shape((32, 256), F32),
            shape((1, 32), F32), shape((1, 256), F32), shape((1, 256), F32), shape((1024, 128), F32),
        ),
        in_specs=[pl.BlockSpec(memory_space=pl.ANY)] * 3,
        out_specs=(pl.BlockSpec(memory_space=pl.ANY),) + (vmem,) * 7,
        scratch_shapes=[v((32, 8, 128), F32), v((512, 256), BF16), pltpu.SemaphoreType.DMA((3,))],
        compiler_params=pltpu.CompilerParams(vmem_limit_bytes=58 * 1024 * 1024),
        name="lay_out",
    )(ag, sf, wg)
    return (
        ag.reshape(128, 8, 256), lw.T, lbg.reshape(32), rw.T, rbg.reshape(32), gain.reshape(256), shift.reshape(256), ow,
    )


def solution(mesh):
    placed = (P("depth", ("row", "col"), None),) + (P(),) * 9 + (P("row", "col", None),)
    return jax.shard_map(
        body,
        mesh=mesh,
        in_specs=placed,
        out_specs=(P("depth", ("row", "col"), None),) + (P(),) * 7,
        check_vma=False,
    )
```

```python
import functools

import jax
import jax.numpy as jnp
from jax import lax
from jax.experimental import pallas as pl
from jax.experimental.pallas import tpu as pltpu
from jax.sharding import PartitionSpec as P

F32, BF16 = jnp.float32, jnp.bfloat16
MESH = pl.DeviceIdType.MESH
NT = (((1,), (1,)), ((), ()))
TN = (((0,), (0,)), ((), ()))
PAIR, OTHER, LEFT, RIGHT, RSUM, RSUM2, LSUM = range(7)
W1, W2, W3, S1, S2, S3 = range(6)


def dot(a, b):
    return jnp.dot(a, b, preferred_element_type=F32)


def dot_nt(a, b, **kw):
    return lax.dot_general(a, b, NT, preferred_element_type=F32, **kw)


def main_kernel(
    x_any, seq_ref, res_ref, res_s, gain_ref, shift_ref, wl_ref, lb_ref, wr_ref, rb_ref, ow_any, pair_any,
    ag_any, sf_ref, wg_ref,
    pair_ref, x_ref, ow_ref, ag_ref, inv1, xf, unit, norm, istd, ngrad, wt, bias, wf, wp, ps, scb, bd, og, outer, lb, lt, rf, rbuf, rt,
    rss, rsr, lss, lsr, lsf, wga, w1s, w1r, w2, w3, wgt, extra, s1s, s1r, s2, s3,
    send_sem, recv_sem, group_send, group_recv, local_sems,
):
    depth, row, col = lax.axis_index("depth"), lax.axis_index("row"), lax.axis_index("col")
    z, h = lax.div(row, 2), lax.rem(row, 2)
    q = h * 4 + col
    core = lax.rem(depth, 2)

    loads = [
        pltpu.make_async_copy(pair_any.at[pl.ds(core * 16, 16)], pair_ref, local_sems.at[0]),
        pltpu.make_async_copy(x_any, x_ref, local_sems.at[1]),
        pltpu.make_async_copy(ow_any, ow_ref, local_sems.at[2]),
    ]
    for load in loads:
        load.start()

    def zpeer(k):
        t = lax.rem(z + k, 8)
        return t, (depth, t * 2 + h, col)

    def qpeer(k):
        t = lax.rem(q + k, 8)
        return t, (depth, z * 2 + lax.div(t, 4), lax.rem(t, 4))

    g = depth * 8 + q

    def gpeer(k):
        t = lax.rem(g + k, 32)
        u = lax.rem(t, 8)
        return t, (lax.div(t, 8), z * 2 + lax.div(u, 4), lax.rem(u, 4))

    def copy(which, k, src, dst, device):
        return pltpu.make_async_remote_copy(
            src_ref=src, dst_ref=dst, send_sem=send_sem.at[which, k], recv_sem=recv_sem.at[which, k],
            device_id=device, device_id_type=MESH,
        )

    def pair_copy(k):
        t, device = qpeer(k)
        return copy(PAIR, k, ps.at[t], scb.at[core, col, h], device)

    def other_copy(k):
        t = lax.rem(q + 8 - k, 8)
        block = scb.at[core, lax.rem(t, 4), lax.div(t, 4)]
        return copy(OTHER, k, block, block, (depth + 1 - 2 * core, row, col))

    def left_copy(k):
        block = lb.at[pl.ds(pl.multiple_of(q * 256, 256), 256)]
        return copy(LEFT, k, block, block, qpeer(k)[1])

    def right_copy(n):
        to = (1, 7, 2, 6, 7, 1, 6, 2)[n]
        whose = (0, 0, 0, 0, 2, 6, 2, 6)[n]
        block = rbuf.at[lax.rem(z + whose, 8)]
        if n >= 6:
            block = block.at[pl.ds((n - 6) * 128, 128)]
        return copy(RIGHT, n, block, block, zpeer(to)[1])

    def rsum_copy(n, part):
        to = (1, 7, 1, 7, 2, 6)[n]
        whose = (1, 7, 3, 5, 4, 4)[n]
        half = pl.ds(part * 128, 128)
        return copy(RSUM + part, n, rss.at[lax.rem(z + whose, 8), half], rsr.at[n, half], zpeer(to)[1])

    def rsum_late(n):
        return copy(RSUM, n, rsr.at[n + 2], rsr.at[n], zpeer((2, 6)[n - 6])[1])

    def rsum_all(part):
        return [functools.partial(rsum_copy, n, part) for n in (2, 3, 4 + part, 0, 1)]

    def lsum_copy(k):
        t, device = qpeer(k)
        return copy(LSUM, k, lss.at[t], lsr.at[k], device)

    def group_copy(which, src, dst, device):
        return pltpu.make_async_remote_copy(
            src_ref=src, dst_ref=dst, send_sem=group_send.at[which], recv_sem=group_recv.at[which],
            device_id=device, device_id_type=MESH,
        )

    def scatter_plane(which, src, dst):
        @pl.loop(1, 32)
        def _(k):
            t, device = gpeer(k)
            group_copy(which, src.at[t], dst.at[k], device).start()

    def share_line(which, ref):
        for k in range(1, 8):
            group_copy(which, ref.at[z], ref.at[z], zpeer(k)[1]).start()

    def gather_plane(which, ref):
        @pl.loop(1, 32)
        def _(k):
            group_copy(which, ref.at[g], ref.at[g], gpeer(k)[1]).start()

    def group_wait(which, ref, sems):
        count = ref.shape[0] - 1
        pltpu.make_async_copy(ref.at[pl.ds(1, count)], ref.at[pl.ds(1, count)], sems.at[which]).wait()

    def start(make, count=8):
        for k in range(1, count):
            make(k).start()

    def arrived(make, count=8):
        for k in range(1, count):
            make(k).wait_recv()

    barrier = pltpu.get_barrier_semaphore()
    for k in range(1, 8):
        pl.semaphore_signal(barrier, inc=1, device_id=zpeer(k)[1], device_id_type=MESH)

    @pl.loop(1, 32)
    def _(k):
        pl.semaphore_signal(barrier, inc=1, device_id=gpeer(k)[1], device_id_type=MESH)

    loads[0].wait()
    used = jnp.sum(seq_ref[...].astype(F32), axis=1, keepdims=True)
    res_j = res_ref[:, pl.ds(pl.multiple_of(col * 128, 128), 128)].astype(F32)
    res_j = jnp.broadcast_to(res_j, (128, 128)).T
    inv1[...] = 1.0 / jnp.maximum(used * res_j, 1.0)

    @pl.loop(0, 16, unroll=2)
    def _(i):
        res_i = res_s[row * 32 + core * 16 + i].astype(F32)
        scaled = pair_ref[i].astype(F32) * (inv1[...] * res_i + (1.0 - res_i))
        for t in range(8):
            piece = jnp.concatenate([scaled[t * 8 : t * 8 + 8], scaled[64 + t * 8 : 72 + t * 8]], axis=0)
            ps[t, i] = piece.astype(BF16)

    pl.semaphore_wait(barrier, 38)
    start(pair_copy)
    own_pair = pltpu.make_async_copy(ps.at[q], scb.at[core, col, h], local_sems.at[3])
    own_pair.start()

    pick = lax.broadcasted_iota(jnp.int32, (64, 32), 0) - lax.broadcasted_iota(jnp.int32, (64, 32), 1)
    first, second = (pick == 0).astype(F32), (pick == 32).astype(F32)
    wt[0:32, :] = wl_ref[...]
    wt[32:64, :] = wr_ref[...]
    exact = dict(precision=lax.Precision.HIGHEST)
    bias[...] = dot_nt(first, jnp.broadcast_to(lb_ref[...], (128, 32)), **exact) + dot_nt(
        second, jnp.broadcast_to(rb_ref[...], (128, 32)), **exact
    )
    loads[1].wait()
    for e in range(2):
        xf[e] = x_ref[:, e * 128 : e * 128 + 128].astype(F32)
    seq_row = seq_ref[:, pl.ds(pl.multiple_of(depth * 128, 128), 128)].astype(F32)
    own_first = (row * 4 + col) * 8

    @pl.loop(0, 8, unroll=4)
    def _(r):
        values = jnp.concatenate([xf[e, pl.ds(r, 128, stride=8), :] for e in range(2)], axis=1)
        centred = values - jnp.mean(values, axis=1, keepdims=True)
        inv_std = lax.rsqrt(jnp.mean(centred * centred, axis=1, keepdims=True) + 1e-05)
        units = centred * inv_std
        normed = (units * gain_ref[...] + shift_ref[...]).astype(BF16)
        unit[r] = units
        norm[r] = normed
        istd[r] = jnp.broadcast_to(inv_std, (128, 128))
        mask = seq_row * res_s[own_first + r].astype(F32)
        both = (dot_nt(wt[...], normed) + bias[...]) * mask
        lb[pl.ds(pl.multiple_of(q * 256 + r * 32, 32), 32), :] = both[:32].astype(BF16)
        rf[pl.ds(r, 32, stride=8), :] = both[32:]

    rbuf[z] = rf[...].astype(BF16)
    for n in (2, 3, 0, 1):
        right_copy(n).start()
    start(left_copy)

    loads[2].wait()
    wf[...] = ow_ref[...].astype(F32)
    for d in range(32):
        wp[d // 2 * 32 : d // 2 * 32 + 32, d % 2 * 128 : d % 2 * 128 + 128] = wf[pl.ds(d, 32, stride=32), :].astype(BF16)

    @pl.loop(0, 64)
    def _(i):
        bd[i] = jnp.zeros((128, 256), BF16)

    own_pair.wait()
    other_copy(0).start()
    for n in (2, 3):
        right_copy(n).wait_recv()
    for n in (4, 5, 6, 7):
        right_copy(n).start()
    for k in range(1, 8):
        pair_copy(k).wait_recv()
        other_copy(k).start()

    def outer_grads(side):
        @pl.loop(0, 16, unroll=8)
        def _(t):
            upper, at = lax.div(t, 8), lax.rem(t, 8) * 2
            i = upper * 32 + side * 16 + at
            for e in range(2):
                block = jnp.concatenate([scb[side, y, upper, at + e] for y in range(4)], axis=0)
                bd[i + e, :64, :128] = block
                bd[i + e, 64:, 128:] = block
            grads = dot_nt(wp[...], bd[pl.ds(i, 2)].reshape(256, 256)).astype(BF16)
            for e in range(2):
                rows = pl.ds(pl.multiple_of((i + e) * 32, 32), 32)
                for p in range(16):
                    og[rows, p * 128 : p * 128 + 128] = grads[p * 32 : p * 32 + 32, e * 128 : e * 128 + 128]

    outer_grads(core)
    for k in range(8):
        other_copy(k).wait_recv()
    outer_grads(1 - core)

    arrived(left_copy)
    for t in range(16):
        block = lb[t * 128 : t * 128 + 128, :].astype(F32)
        lt[:, t * 128 : t * 128 + 128] = block.T.astype(BF16)

    def right_sums(part):
        sums = dot(lt[...], og[:, part * 1024 : part * 1024 + 1024])
        for p in range(8):
            turned = sums[:, p * 128 : p * 128 + 128].T
            at = part * 128 + p * 16
            for t in range(8):
                piece = jnp.concatenate([turned[t * 8 : t * 8 + 8], turned[64 + t * 8 : 72 + t * 8]], axis=0)
                rss[t, at : at + 16, :] = piece.astype(BF16)

    for part in range(2):
        right_sums(part)
        for make in rsum_all(part):
            make().start()

    for n in (0, 1, 4, 5, 6, 7):
        right_copy(n).wait_recv()

    @pl.loop(0, 16)
    def _(p):
        blocks = [rbuf[t, pl.ds(pl.multiple_of(p * 16, 16), 16), :].astype(F32) for t in range(8)]
        rows = [block[:8] for block in blocks] + [block[8:] for block in blocks]
        rt[pl.ds(pl.multiple_of(p * 128, 128), 128), :] = jnp.concatenate(rows, axis=0).astype(BF16)

    def left_sum(t):
        at = pl.ds(pl.multiple_of(t * 256, 256), 256)
        lss[t] = dot(og[at, :], rt[...]).astype(BF16)

    @pl.loop(1, 8)
    def _(k):
        left_sum(lax.rem(q + k, 8))
        lsum_copy(k).start()

    left_sum(q)

    for part in range(2):
        for make in rsum_all(part)[:3]:
            make().wait_recv()
    for n in range(2):
        half = pl.ds(n * 128, 128)
        rsr[8 + n] = (rss[lax.rem(z + (2, 6)[n], 8)].astype(F32) + rsr[2 + n].astype(F32)).astype(BF16)
        rsr[8 + n, half] = (rsr[8 + n, half].astype(F32) + rsr[4 + n, half].astype(F32)).astype(BF16)
        rsum_late(6 + n).start()

    @pl.loop(0, 8, unroll=4)
    def _(n):
        at = pl.ds(pl.multiple_of(n * 256, 256), 256)
        for m in range(4):
            product = dot_nt(lb[m * 512 : m * 512 + 512, :], rt[at, :])
            outer[m * 512 : m * 512 + 512, at] = product.astype(BF16)

    wga[...] = jnp.zeros_like(wga)

    @pl.loop(0, 4)
    def _(t):
        blocks = [outer[pl.ds(pl.multiple_of((16 * t + e) * 32, 32), 32), :] for e in range(16)]
        rows = [
            jnp.concatenate([block[:, p * 128 : p * 128 + 128] for block in blocks], axis=1) for p in range(16)
        ]
        wga[...] += dot(jnp.concatenate(rows, axis=0), bd[pl.ds(16 * t, 16)].reshape(2048, 256))

    for t in range(32):
        w1s[t] = wga[t * 16 : t * 16 + 16, :].astype(BF16)
    scatter_plane(W1, w1s, w1r)

    arrived(lsum_copy)
    total = lss[q].astype(F32)
    for k in range(1, 8):
        total = total + lsr[k].astype(F32)
    lsf[...] = total
    for part in range(2):
        for make in rsum_all(part)[3:]:
            make().wait_recv()
    total = rss[z].astype(F32)
    for n in (0, 1, 6, 7):
        if n >= 6:
            rsum_late(n).wait_recv()
        total = total + rsr[n].astype(F32)
    rf[...] = total

    wgt[...] = jnp.zeros_like(wgt)
    extra[...] = jnp.zeros_like(extra)

    @pl.loop(0, 8, unroll=4)
    def _(r):
        mask = seq_row * res_s[own_first + r].astype(F32)
        sides = [lsf[pl.ds(pl.multiple_of(r * 32, 32), 32), :], rf[pl.ds(r, 32, stride=8), :]]
        pre = (jnp.concatenate(sides, axis=0) * mask).astype(BF16)
        grad = lax.dot_general(pre, wt[...], TN, preferred_element_type=F32)
        ngrad[r] = grad
        wgt[...] += dot(pre, norm[r])
        extra[0:1, :] += jnp.sum(grad * unit[r], axis=0, keepdims=True)
        extra[1:2, :] += jnp.sum(grad, axis=0, keepdims=True)
        extra[2:3, 0:64] += dot_nt(jnp.ones((8, 128), BF16), pre)[0:1]

    upper = lax.broadcasted_iota(jnp.int32, (8, 128), 0) < 4
    for t in range(16):
        tile = wgt[t // 2 * 8 : t // 2 * 8 + 8, t % 2 * 128 : t % 2 * 128 + 128]
        s1s[2 * t] = jnp.where(upper, tile, 0.0)
        s1s[2 * t + 1] = jnp.where(upper, 0.0, tile)
    s1s[0, 4:5, :] = extra[0:1, :128]
    s1s[1, 0:1, :] = extra[0:1, 128:]
    s1s[2, 4:5, :] = extra[1:2, :128]
    s1s[3, 0:1, :] = extra[1:2, 128:]
    s1s[4, 4:5, :] = extra[2:3, :128]
    scatter_plane(S1, s1s, s1r)

    def input_grad(r):
        units = unit[r]
        weighted = ngrad[r] * gain_ref[...]
        mean = jnp.mean(weighted, axis=1, keepdims=True)
        along = jnp.mean(weighted * units, axis=1, keepdims=True)
        scale = jnp.concatenate([istd[r], istd[r]], axis=1)
        result = scale * (weighted - mean - units * along)
        for e in range(2):
            xf[e, pl.ds(r, 128, stride=8), :] = result[:, e * 128 : e * 128 + 128]

    def summed(ref, count, first):
        total = first
        for k in range(1, count):
            total = total + ref[k].astype(F32)
        return total

    @pl.loop(0, 4, unroll=4)
    def _(r):
        input_grad(r)

    group_wait(W1, w1r, group_recv)
    w2[z] = summed(w1r, 32, wga[pl.ds(pl.multiple_of(g * 16, 16), 16), :]).astype(BF16)
    share_line(W2, w2)
    group_wait(S1, s1r, group_recv)
    s2[z] = summed(s1r, 32, s1s[g])
    share_line(S2, s2)

    @pl.loop(4, 8, unroll=4)
    def _(r):
        input_grad(r)

    for e in range(2):
        ag_ref[:, e * 128 : e * 128 + 128] = xf[e].astype(BF16)
    store = pltpu.make_async_copy(ag_ref, ag_any, local_sems.at[4])
    store.start()

    group_wait(W2, w2, group_recv)
    w3[g] = summed(w2, 8, w2[0].astype(F32)).astype(BF16)
    gather_plane(W3, w3)
    group_wait(S2, s2, group_recv)
    s3[g] = summed(s2, 8, s2[0])
    gather_plane(S3, s3)

    for make in (pair_copy, left_copy, lsum_copy):
        for k in range(1, 8):
            make(k).wait_send()
    for n in range(8):
        other_copy(n).wait_send()
        right_copy(n).wait_send()
    for make in rsum_all(0) + rsum_all(1):
        make().wait_send()
    for n in (6, 7):
        rsum_late(n).wait_send()
    for which, ref in ((W1, w1s), (W2, w2), (W3, w3), (S1, s1s), (S2, s2), (S3, s3)):
        group_wait(which, ref, group_send)

    group_wait(W3, w3, group_recv)
    for t in range(32):
        wg_ref[t * 16 : t * 16 + 16, :] = w3[t]
    group_wait(S3, s3, group_recv)
    sf_ref[...] = s3[...]
    store.wait()


def last_kernel(
    ag_any, sf_any, wg_any, ag_out, lw_ref, lb_ref, rw_ref, rb_ref, gain_ref, shift_ref, ow_ref, sf, wg, ag, sems
):
    moves = [
        pltpu.make_async_copy(src, dst, sems.at[n])
        for n, (src, dst) in enumerate(((ag_any, ag), (wg_any, wg), (sf_any, sf), (ag, ag_out)))
    ]
    for move in moves[:3]:
        move.start()
    moves[0].wait()
    moves[3].start()
    moves[1].wait()
    for d in range(32):
        tile = wg[d // 2 * 32 : d // 2 * 32 + 32, d % 2 * 128 : d % 2 * 128 + 128]
        ow_ref[pl.ds(d, 32, stride=32), :] = tile.astype(F32)
    moves[2].wait()
    upper = lax.broadcasted_iota(jnp.int32, (8, 128), 0) < 4
    for t in range(16):
        tile = jnp.where(upper, sf[2 * t], sf[2 * t + 1])
        side, row, lane = (lw_ref, rw_ref)[t // 8], t % 8 // 2 * 8, t % 2 * 128
        side[row : row + 8, lane : lane + 128] = tile
    gain_ref[:, :128] = sf[0, 4:5, :]
    gain_ref[:, 128:] = sf[1, 0:1, :]
    shift_ref[:, :128] = sf[2, 4:5, :]
    shift_ref[:, 128:] = sf[3, 0:1, :]
    lb_ref[...] = sf[4, 4:5, 0:32]
    rb_ref[...] = sf[4, 4:5, 32:64]
    moves[3].wait()


def body(
    alignment, seq_mask, residue_mask, layer_norm_gain, layer_norm_bias, left_projection_weight, left_bias,
    right_projection_weight, right_bias, out_weight, pair_grad,
):
    vmem = pl.BlockSpec(memory_space=pltpu.VMEM)
    smem = pl.BlockSpec(memory_space=pltpu.SMEM)
    hbm = pl.BlockSpec(memory_space=pl.ANY)
    v = pltpu.VMEM
    shape = jax.ShapeDtypeStruct
    scratch = [
        v((16, 128, 128), BF16),
        v((1024, 256), BF16),
        v((1024, 128), BF16),
        v((1024, 256), BF16),
        v((128, 128), F32),
        v((2, 1024, 128), F32),
        v((8, 128, 256), F32),
        v((8, 128, 256), BF16),
        v((8, 128, 128), F32),
        v((8, 128, 256), F32),
        v((64, 256), BF16),
        v((64, 128), F32),
        v((1024, 128), F32),
        v((512, 256), BF16),
        v((8, 16, 16, 128), BF16),
        v((2, 4, 2, 16, 16, 128), BF16),
        v((64, 128, 256), BF16),
        v((2048, 2048), BF16),
        v((2048, 2048), BF16),
        v((2048, 128), BF16),
        v((128, 2048), BF16),
        v((256, 128), F32),
        v((8, 256, 128), BF16),
        v((2048, 128), BF16),
        v((8, 256, 128), BF16),
        v((10, 256, 128), BF16),
        v((8, 256, 128), BF16),
        v((8, 256, 128), BF16),
        v((256, 128), F32),
        v((512, 256), F32),
        v((32, 16, 256), BF16),
        v((32, 16, 256), BF16),
        v((8, 16, 256), BF16),
        v((32, 16, 256), BF16),
        v((64, 256), F32),
        v((8, 256), F32),
        v((32, 8, 128), F32),
        v((32, 8, 128), F32),
        v((8, 8, 128), F32),
        v((32, 8, 128), F32),
        pltpu.SemaphoreType.DMA((7, 8)),
        pltpu.SemaphoreType.DMA((7, 8)),
        pltpu.SemaphoreType.DMA((6,)),
        pltpu.SemaphoreType.DMA((6,)),
        pltpu.SemaphoreType.DMA((5,)),
    ]
    ag, sf, wg = pl.pallas_call(
        main_kernel,
        out_shape=(shape((1024, 256), BF16), shape((32, 8, 128), F32), shape((512, 256), BF16)),
        in_specs=[hbm] + [vmem] * 2 + [smem] + [vmem] * 6 + [hbm] * 2,
        out_specs=(hbm, vmem, vmem),
        scratch_shapes=scratch,
        compiler_params=pltpu.CompilerParams(
            collective_id=0, has_side_effects=True, vmem_limit_bytes=58 * 1024 * 1024
        ),
        name="pair_backward",
    )(
        alignment.reshape(1024, 256), seq_mask.reshape(1, 512), residue_mask.reshape(1, 512), residue_mask,
        layer_norm_gain.reshape(1, 256), layer_norm_bias.reshape(1, 256), left_projection_weight.T,
        left_bias.reshape(1, 32), right_projection_weight.T, right_bias.reshape(1, 32), out_weight, pair_grad,
    )
    ag, lw, lbg, rw, rbg, gain, shift, ow = pl.pallas_call(
        last_kernel,
        out_shape=(
            shape((1024, 256), BF16), shape((32, 256), F32), shape((1, 32), F32), shape((32, 256), F32),
            shape((1, 32), F32), shape((1, 256), F32), shape((1, 256), F32), shape((1024, 128), F32),
        ),
        in_specs=[pl.BlockSpec(memory_space=pl.ANY)] * 3,
        out_specs=(pl.BlockSpec(memory_space=pl.ANY),) + (vmem,) * 7,
        scratch_shapes=[v((32, 8, 128), F32), v((512, 256), BF16), v((1024, 256), BF16), pltpu.SemaphoreType.DMA((4,))],
        compiler_params=pltpu.CompilerParams(vmem_limit_bytes=58 * 1024 * 1024),
        name="lay_out",
    )(ag, sf, wg)
    return (
        ag.reshape(128, 8, 256), lw.T, lbg.reshape(32), rw.T, rbg.reshape(32), gain.reshape(256), shift.reshape(256), ow,
    )


def solution(mesh):
    placed = (P("depth", ("row", "col"), None),) + (P(),) * 9 + (P("row", "col", None),)
    return jax.shard_map(
        body,
        mesh=mesh,
        in_specs=placed,
        out_specs=(P("depth", ("row", "col"), None),) + (P(),) * 7,
        check_vma=False,
    )
```

```python
import functools

import jax
import jax.numpy as jnp
from jax import lax
from jax.experimental import pallas as pl
from jax.experimental.pallas import tpu as pltpu
from jax.sharding import PartitionSpec as P

F32, BF16 = jnp.float32, jnp.bfloat16
MESH = pl.DeviceIdType.MESH
NT = (((1,), (1,)), ((), ()))
TN = (((0,), (0,)), ((), ()))
PAIR, OTHER, LEFT, RIGHT, RSUM, RSUM2, LSUM = range(7)
W1, W2, W3, S1, S2, S3 = range(6)


def dot(a, b):
    return jnp.dot(a, b, preferred_element_type=F32)


def dot_nt(a, b, **kw):
    return lax.dot_general(a, b, NT, preferred_element_type=F32, **kw)


def main_kernel(
    x_any, seq_ref, res_ref, res_s, gain_ref, shift_ref, wl_ref, lb_ref, wr_ref, rb_ref, ow_any, pair_any,
    ag_any, sf_any, wg_any,
    pair_ref, x_ref, ow_ref, ag_ref, inv1, xf, unit, norm, istd, ngrad, wt, bias, wf, wp, ps, scb, bd, og, outer, lb, lt, rf, rbuf, rt,
    rss, rsr, lss, lsr, lsf, wga, w1s, w1r, w2, w3, wgt, extra, s1s, s1r, s2, s3,
    send_sem, recv_sem, group_send, group_recv, local_sems,
):
    depth, row, col = lax.axis_index("depth"), lax.axis_index("row"), lax.axis_index("col")
    z, h = lax.div(row, 2), lax.rem(row, 2)
    q = h * 4 + col
    core = lax.rem(depth, 2)

    loads = [
        pltpu.make_async_copy(pair_any.at[pl.ds(core * 16, 16)], pair_ref, local_sems.at[0]),
        pltpu.make_async_copy(x_any, x_ref, local_sems.at[1]),
        pltpu.make_async_copy(ow_any, ow_ref, local_sems.at[2]),
    ]
    for load in loads:
        load.start()

    def zpeer(k):
        t = lax.rem(z + k, 8)
        return t, (depth, t * 2 + h, col)

    def qpeer(k):
        t = lax.rem(q + k, 8)
        return t, (depth, z * 2 + lax.div(t, 4), lax.rem(t, 4))

    g = depth * 8 + q

    steps = sorted(
        [(n // 16, n // 8 % 2, n // 4 % 2, n % 4) for n in range(1, 32)],
        key=lambda step: -(step[0] + (0, 2, 1, 1)[step[1] + 2 * step[2]] + (0, 1, 2, 1)[step[3]]),
    )

    def gpeer(k):
        side, over, low, along = steps[k - 1]
        to_core, to_low = lax.rem(core + side, 2), lax.rem(lax.div(depth, 2) + low, 2)
        to_h, to_col = lax.rem(h + over, 2), lax.rem(col + along, 4)
        to_depth = to_low * 2 + to_core
        return to_depth * 8 + to_h * 4 + to_col, (to_depth, z * 2 + to_h, to_col)

    def copy(which, k, src, dst, device):
        return pltpu.make_async_remote_copy(
            src_ref=src, dst_ref=dst, send_sem=send_sem.at[which, k], recv_sem=recv_sem.at[which, k],
            device_id=device, device_id_type=MESH,
        )

    def pair_copy(k):
        t, device = qpeer(k)
        return copy(PAIR, k, ps.at[t], scb.at[core, col, h], device)

    def other_copy(k):
        t = lax.rem(q + 8 - k, 8)
        block = scb.at[core, lax.rem(t, 4), lax.div(t, 4)]
        return copy(OTHER, k, block, block, (depth + 1 - 2 * core, row, col))

    def left_copy(k):
        block = lb.at[pl.ds(pl.multiple_of(q * 256, 256), 256)]
        return copy(LEFT, k, block, block, qpeer(k)[1])

    def right_copy(n):
        to = (1, 7, 2, 6, 7, 1, 6, 2)[n]
        whose = (0, 0, 0, 0, 2, 6, 2, 6)[n]
        block = rbuf.at[lax.rem(z + whose, 8)]
        if n >= 6:
            block = block.at[pl.ds((n - 6) * 128, 128)]
        return copy(RIGHT, n, block, block, zpeer(to)[1])

    def rsum_copy(n, part):
        to = (1, 7, 1, 7, 2, 6)[n]
        whose = (1, 7, 3, 5, 4, 4)[n]
        half = pl.ds(part * 128, 128)
        return copy(RSUM + part, n, rss.at[lax.rem(z + whose, 8), half], rsr.at[n, half], zpeer(to)[1])

    def rsum_late(n, part):
        half = pl.ds(part * 128, 128)
        return copy(RSUM + part, n, rsr.at[n + 2, half], rsr.at[n, half], zpeer((2, 6)[n - 6])[1])

    def rsum_all(part):
        return [functools.partial(rsum_copy, n, part) for n in (2, 3, 4 + part, 0, 1)]

    def lsum_copy(k):
        t, device = qpeer(k)
        return copy(LSUM, k, lss.at[t], lsr.at[k], device)

    def group_copy(which, src, dst, device):
        return pltpu.make_async_remote_copy(
            src_ref=src, dst_ref=dst, send_sem=group_send.at[which], recv_sem=group_recv.at[which],
            device_id=device, device_id_type=MESH,
        )

    def scatter_plane(which, src, dst):
        for k in range(1, 32):
            t, device = gpeer(k)
            group_copy(which, src.at[t], dst.at[k], device).start()

    def share_line(which, ref):
        for k in (4, 3, 5, 2, 6, 1, 7):
            group_copy(which, ref.at[z], ref.at[z], zpeer(k)[1]).start()

    def gather_plane(which, ref):
        for k in range(1, 32):
            group_copy(which, ref.at[g], ref.at[g], gpeer(k)[1]).start()

    def group_wait(which, ref, sems):
        count = ref.shape[0] - 1
        pltpu.make_async_copy(ref.at[pl.ds(1, count)], ref.at[pl.ds(1, count)], sems.at[which]).wait()

    def start(make, count=8):
        for k in range(1, count):
            make(k).start()

    def arrived(make, count=8):
        for k in range(1, count):
            make(k).wait_recv()

    barrier = pltpu.get_barrier_semaphore()
    for k in range(1, 8):
        pl.semaphore_signal(barrier, inc=1, device_id=zpeer(k)[1], device_id_type=MESH)

    for k in range(1, 32):
        pl.semaphore_signal(barrier, inc=1, device_id=gpeer(k)[1], device_id_type=MESH)

    loads[0].wait()
    used = jnp.sum(seq_ref[...].astype(F32), axis=1, keepdims=True)
    res_j = res_ref[:, pl.ds(pl.multiple_of(col * 128, 128), 128)].astype(F32)
    res_j = jnp.broadcast_to(res_j, (128, 128)).T
    inv1[...] = 1.0 / jnp.maximum(used * res_j, 1.0)

    @pl.loop(0, 16, unroll=2)
    def _(i):
        res_i = res_s[row * 32 + core * 16 + i].astype(F32)
        scaled = pair_ref[i].astype(F32) * (inv1[...] * res_i + (1.0 - res_i))
        for t in range(8):
            piece = jnp.concatenate([scaled[t * 8 : t * 8 + 8], scaled[64 + t * 8 : 72 + t * 8]], axis=0)
            ps[t, i] = piece.astype(BF16)

    pl.semaphore_wait(barrier, 38)
    start(pair_copy)
    own_pair = pltpu.make_async_copy(ps.at[q], scb.at[core, col, h], local_sems.at[3])
    own_pair.start()

    pick = lax.broadcasted_iota(jnp.int32, (64, 32), 0) - lax.broadcasted_iota(jnp.int32, (64, 32), 1)
    first, second = (pick == 0).astype(F32), (pick == 32).astype(F32)
    wt[0:32, :] = wl_ref[...]
    wt[32:64, :] = wr_ref[...]
    exact = dict(precision=lax.Precision.HIGHEST)
    bias[...] = dot_nt(first, jnp.broadcast_to(lb_ref[...], (128, 32)), **exact) + dot_nt(
        second, jnp.broadcast_to(rb_ref[...], (128, 32)), **exact
    )
    loads[1].wait()
    for e in range(2):
        xf[e] = x_ref[:, e * 128 : e * 128 + 128].astype(F32)
    seq_row = seq_ref[:, pl.ds(pl.multiple_of(depth * 128, 128), 128)].astype(F32)
    own_first = (row * 4 + col) * 8

    @pl.loop(0, 8, unroll=4)
    def _(r):
        values = jnp.concatenate([xf[e, pl.ds(r, 128, stride=8), :] for e in range(2)], axis=1)
        centred = values - jnp.mean(values, axis=1, keepdims=True)
        inv_std = lax.rsqrt(jnp.mean(centred * centred, axis=1, keepdims=True) + 1e-05)
        units = centred * inv_std
        normed = (units * gain_ref[...] + shift_ref[...]).astype(BF16)
        unit[r] = units
        norm[r] = normed
        istd[r] = jnp.broadcast_to(inv_std, (128, 128))
        mask = seq_row * res_s[own_first + r].astype(F32)
        both = (dot_nt(wt[...], normed) + bias[...]) * mask
        lb[pl.ds(pl.multiple_of(q * 256 + r * 32, 32), 32), :] = both[:32].astype(BF16)
        rf[pl.ds(r, 32, stride=8), :] = both[32:]

    rbuf[z] = rf[...].astype(BF16)
    for n in (2, 3, 0, 1):
        right_copy(n).start()
    start(left_copy)

    loads[2].wait()
    wf[...] = ow_ref[...].astype(F32)
    for d in range(32):
        wp[d // 2 * 32 : d // 2 * 32 + 32, d % 2 * 128 : d % 2 * 128 + 128] = wf[pl.ds(d, 32, stride=32), :].astype(BF16)

    @pl.loop(0, 64)
    def _(i):
        bd[i] = jnp.zeros((128, 256), BF16)

    own_pair.wait()
    other_copy(0).start()
    for n in (2, 3):
        right_copy(n).wait_recv()
    for n in (4, 5, 6, 7):
        right_copy(n).start()
    for k in range(1, 8):
        pair_copy(k).wait_recv()
        other_copy(k).start()

    def outer_grads(side):
        @pl.loop(0, 16, unroll=8)
        def _(t):
            upper, at = lax.div(t, 8), lax.rem(t, 8) * 2
            i = upper * 32 + side * 16 + at
            for e in range(2):
                block = jnp.concatenate([scb[side, y, upper, at + e] for y in range(4)], axis=0)
                bd[i + e, :64, :128] = block
                bd[i + e, 64:, 128:] = block
            grads = dot_nt(wp[...], bd[pl.ds(i, 2)].reshape(256, 256)).astype(BF16)
            for e in range(2):
                rows = pl.ds(pl.multiple_of((i + e) * 32, 32), 32)
                for p in range(16):
                    og[rows, p * 128 : p * 128 + 128] = grads[p * 32 : p * 32 + 32, e * 128 : e * 128 + 128]

    outer_grads(core)
    for k in range(8):
        other_copy(k).wait_recv()
    outer_grads(1 - core)

    for n in (0, 1, 4, 5, 6, 7):
        right_copy(n).wait_recv()

    @pl.loop(0, 16, unroll=4)
    def _(p):
        blocks = [rbuf[t, pl.ds(pl.multiple_of(p * 16, 16), 16), :].astype(F32) for t in range(8)]
        rows = [block[:8] for block in blocks] + [block[8:] for block in blocks]
        rt[pl.ds(pl.multiple_of(p * 128, 128), 128), :] = jnp.concatenate(rows, axis=0).astype(BF16)

    def products(t):
        at = pl.multiple_of(t * 256, 256)
        block = lb[pl.ds(at, 256), :]
        outer[pl.ds(at, 256), :] = dot_nt(block, rt[...]).astype(BF16)
        for e in range(2):
            lt[:, pl.ds(at + e * 128, 128)] = block[e * 128 : e * 128 + 128].astype(F32).T.astype(BF16)

    products(q)

    @pl.loop(1, 8)
    def _(k):
        left_copy(k).wait_recv()
        products(lax.rem(q + 8 - k, 8))

    def right_sums(part):
        sums = dot(lt[...], og[:, part * 1024 : part * 1024 + 1024])
        for p in range(8):
            turned = sums[:, p * 128 : p * 128 + 128].T
            at = part * 128 + p * 16
            for t in range(8):
                piece = jnp.concatenate([turned[t * 8 : t * 8 + 8], turned[64 + t * 8 : 72 + t * 8]], axis=0)
                rss[t, at : at + 16, :] = piece.astype(BF16)

    for part in range(2):
        right_sums(part)
        for make in rsum_all(part)[:3]:
            make().start()
    for part in range(2):
        for make in rsum_all(part)[3:]:
            make().start()

    def left_sum(t):
        at = pl.ds(pl.multiple_of(t * 256, 256), 256)
        lss[t] = dot(og[at, :], rt[...]).astype(BF16)

    def send_left(k):
        left_sum(lax.rem(q + k, 8))
        lsum_copy(k).start()

    def relay(part):
        half = pl.ds(part * 128, 128)
        for make in rsum_all(part)[:3]:
            make().wait_recv()
        for n in range(2):
            total = rss[lax.rem(z + (2, 6)[n], 8), half].astype(F32) + rsr[2 + n, half].astype(F32)
            if n == part:
                total = total + rsr[4 + n, half].astype(F32)
            rsr[8 + n, half] = total.astype(BF16)
            rsum_late(6 + n, part).start()

    @pl.loop(1, 5)
    def _(k):
        send_left(k)

    relay(0)

    @pl.loop(5, 8)
    def _(k):
        send_left(k)

    relay(1)
    left_sum(q)

    wga[...] = jnp.zeros_like(wga)

    @pl.loop(0, 4)
    def _(t):
        blocks = [outer[pl.ds(pl.multiple_of((16 * t + e) * 32, 32), 32), :] for e in range(16)]
        rows = [
            jnp.concatenate([block[:, p * 128 : p * 128 + 128] for block in blocks], axis=1) for p in range(16)
        ]
        wga[...] += dot(jnp.concatenate(rows, axis=0), bd[pl.ds(16 * t, 16)].reshape(2048, 256))

    for t in range(32):
        w1s[t] = wga[t * 16 : t * 16 + 16, :].astype(BF16)
    scatter_plane(W1, w1s, w1r)

    arrived(lsum_copy)
    total = lss[q].astype(F32)
    for k in range(1, 8):
        total = total + lsr[k].astype(F32)
    lsf[...] = total
    for part in range(2):
        for make in rsum_all(part)[3:]:
            make().wait_recv()
    total = rss[z].astype(F32)
    for n in (0, 1, 6, 7):
        if n >= 6:
            rsum_late(n, 0).wait_recv()
            rsum_late(n, 1).wait_recv()
        total = total + rsr[n].astype(F32)
    rf[...] = total

    wgt[...] = jnp.zeros_like(wgt)
    extra[...] = jnp.zeros_like(extra)

    @pl.loop(0, 8, unroll=4)
    def _(r):
        mask = seq_row * res_s[own_first + r].astype(F32)
        sides = [lsf[pl.ds(pl.multiple_of(r * 32, 32), 32), :], rf[pl.ds(r, 32, stride=8), :]]
        pre = (jnp.concatenate(sides, axis=0) * mask).astype(BF16)
        grad = lax.dot_general(pre, wt[...], TN, preferred_element_type=F32)
        ngrad[r] = grad
        wgt[...] += dot(pre, norm[r])
        extra[0:1, :] += jnp.sum(grad * unit[r], axis=0, keepdims=True)
        extra[1:2, :] += jnp.sum(grad, axis=0, keepdims=True)
        extra[2:3, 0:64] += dot_nt(jnp.ones((8, 128), BF16), pre)[0:1]

    upper = lax.broadcasted_iota(jnp.int32, (8, 128), 0) < 4
    for t in range(16):
        tile = wgt[t // 2 * 8 : t // 2 * 8 + 8, t % 2 * 128 : t % 2 * 128 + 128]
        s1s[2 * t] = jnp.where(upper, tile, 0.0)
        s1s[2 * t + 1] = jnp.where(upper, 0.0, tile)
    s1s[0, 4:5, :] = extra[0:1, :128]
    s1s[1, 0:1, :] = extra[0:1, 128:]
    s1s[2, 4:5, :] = extra[1:2, :128]
    s1s[3, 0:1, :] = extra[1:2, 128:]
    s1s[4, 4:5, :] = extra[2:3, :128]
    scatter_plane(S1, s1s, s1r)

    def input_grad(r):
        units = unit[r]
        weighted = ngrad[r] * gain_ref[...]
        mean = jnp.mean(weighted, axis=1, keepdims=True)
        along = jnp.mean(weighted * units, axis=1, keepdims=True)
        scale = jnp.concatenate([istd[r], istd[r]], axis=1)
        result = scale * (weighted - mean - units * along)
        for e in range(2):
            xf[e, pl.ds(r, 128, stride=8), :] = result[:, e * 128 : e * 128 + 128]

    def summed(ref, count, first):
        total = first
        for k in range(1, count):
            total = total + ref[k].astype(F32)
        return total

    @pl.loop(0, 4, unroll=4)
    def _(r):
        input_grad(r)

    group_wait(W1, w1r, group_recv)
    w2[z] = summed(w1r, 32, wga[pl.ds(pl.multiple_of(g * 16, 16), 16), :]).astype(BF16)
    share_line(W2, w2)
    group_wait(S1, s1r, group_recv)
    s2[z] = summed(s1r, 32, s1s[g])
    share_line(S2, s2)

    @pl.loop(4, 8, unroll=4)
    def _(r):
        input_grad(r)

    for e in range(2):
        ag_ref[:, e * 128 : e * 128 + 128] = xf[e].astype(BF16)
    store = pltpu.make_async_copy(ag_ref, ag_any, local_sems.at[4])
    store.start()

    group_wait(W2, w2, group_recv)
    w3[g] = summed(w2, 8, w2[0].astype(F32)).astype(BF16)
    gather_plane(W3, w3)
    group_wait(S2, s2, group_recv)
    s3[g] = summed(s2, 8, s2[0])
    gather_plane(S3, s3)

    for make in (pair_copy, left_copy, lsum_copy):
        for k in range(1, 8):
            make(k).wait_send()
    for n in range(8):
        other_copy(n).wait_send()
        right_copy(n).wait_send()
    for make in rsum_all(0) + rsum_all(1):
        make().wait_send()
    for n in (6, 7):
        rsum_late(n, 0).wait_send()
        rsum_late(n, 1).wait_send()
    for which, ref in ((W1, w1s), (W2, w2), (W3, w3), (S1, s1s), (S2, s2), (S3, s3)):
        group_wait(which, ref, group_send)

    group_wait(W3, w3, group_recv)
    store_wg = pltpu.make_async_copy(w3, wg_any, local_sems.at[0])
    store_wg.start()
    group_wait(S3, s3, group_recv)
    store_sf = pltpu.make_async_copy(s3, sf_any, local_sems.at[1])
    store_sf.start()
    store.wait()
    store_wg.wait()
    store_sf.wait()


def last_kernel(
    ag_any, sf_any, wg_any, ag_out, lw_ref, lb_ref, rw_ref, rb_ref, gain_ref, shift_ref, ow_ref, sf, wg, ag, sems
):
    moves = [
        pltpu.make_async_copy(src, dst, sems.at[n])
        for n, (src, dst) in enumerate(((ag_any, ag), (wg_any, wg), (sf_any, sf), (ag, ag_out)))
    ]
    for move in moves[:3]:
        move.start()
    moves[0].wait()
    moves[3].start()
    moves[1].wait()
    for d in range(32):
        tile = wg[d // 2 * 2 : d // 2 * 2 + 2, :, d % 2 * 128 : d % 2 * 128 + 128].reshape(32, 128)
        ow_ref[pl.ds(d, 32, stride=32), :] = tile.astype(F32)
    moves[2].wait()
    upper = lax.broadcasted_iota(jnp.int32, (8, 128), 0) < 4
    for t in range(16):
        tile = jnp.where(upper, sf[2 * t], sf[2 * t + 1])
        side, row, lane = (lw_ref, rw_ref)[t // 8], t % 8 // 2 * 8, t % 2 * 128
        side[row : row + 8, lane : lane + 128] = tile
    gain_ref[:, :128] = sf[0, 4:5, :]
    gain_ref[:, 128:] = sf[1, 0:1, :]
    shift_ref[:, :128] = sf[2, 4:5, :]
    shift_ref[:, 128:] = sf[3, 0:1, :]
    lb_ref[...] = sf[4, 4:5, 0:32]
    rb_ref[...] = sf[4, 4:5, 32:64]
    moves[3].wait()


def body(
    alignment, seq_mask, residue_mask, layer_norm_gain, layer_norm_bias, left_projection_weight, left_bias,
    right_projection_weight, right_bias, out_weight, pair_grad,
):
    vmem = pl.BlockSpec(memory_space=pltpu.VMEM)
    smem = pl.BlockSpec(memory_space=pltpu.SMEM)
    hbm = pl.BlockSpec(memory_space=pl.ANY)
    v = pltpu.VMEM
    shape = jax.ShapeDtypeStruct
    scratch = [
        v((16, 128, 128), BF16),
        v((1024, 256), BF16),
        v((1024, 128), BF16),
        v((1024, 256), BF16),
        v((128, 128), F32),
        v((2, 1024, 128), F32),
        v((8, 128, 256), F32),
        v((8, 128, 256), BF16),
        v((8, 128, 128), F32),
        v((8, 128, 256), F32),
        v((64, 256), BF16),
        v((64, 128), F32),
        v((1024, 128), F32),
        v((512, 256), BF16),
        v((8, 16, 16, 128), BF16),
        v((2, 4, 2, 16, 16, 128), BF16),
        v((64, 128, 256), BF16),
        v((2048, 2048), BF16),
        v((2048, 2048), BF16),
        v((2048, 128), BF16),
        v((128, 2048), BF16),
        v((256, 128), F32),
        v((8, 256, 128), BF16),
        v((2048, 128), BF16),
        v((8, 256, 128), BF16),
        v((10, 256, 128), BF16),
        v((8, 256, 128), BF16),
        v((8, 256, 128), BF16),
        v((256, 128), F32),
        v((512, 256), F32),
        v((32, 16, 256), BF16),
        v((32, 16, 256), BF16),
        v((8, 16, 256), BF16),
        v((32, 16, 256), BF16),
        v((64, 256), F32),
        v((8, 256), F32),
        v((32, 8, 128), F32),
        v((32, 8, 128), F32),
        v((8, 8, 128), F32),
        v((32, 8, 128), F32),
        pltpu.SemaphoreType.DMA((7, 8)),
        pltpu.SemaphoreType.DMA((7, 8)),
        pltpu.SemaphoreType.DMA((6,)),
        pltpu.SemaphoreType.DMA((6,)),
        pltpu.SemaphoreType.DMA((5,)),
    ]
    ag, sf, wg = pl.pallas_call(
        main_kernel,
        out_shape=(shape((1024, 256), BF16), shape((32, 8, 128), F32), shape((32, 16, 256), BF16)),
        in_specs=[hbm] + [vmem] * 2 + [smem] + [vmem] * 6 + [hbm] * 2,
        out_specs=(hbm,) * 3,
        scratch_shapes=scratch,
        compiler_params=pltpu.CompilerParams(
            collective_id=0, has_side_effects=True, vmem_limit_bytes=58 * 1024 * 1024
        ),
        name="pair_backward",
    )(
        alignment.reshape(1024, 256), seq_mask.reshape(1, 512), residue_mask.reshape(1, 512), residue_mask,
        layer_norm_gain.reshape(1, 256), layer_norm_bias.reshape(1, 256), left_projection_weight.T,
        left_bias.reshape(1, 32), right_projection_weight.T, right_bias.reshape(1, 32), out_weight, pair_grad,
    )
    ag, lw, lbg, rw, rbg, gain, shift, ow = pl.pallas_call(
        last_kernel,
        out_shape=(
            shape((1024, 256), BF16), shape((32, 256), F32), shape((1, 32), F32), shape((32, 256), F32),
            shape((1, 32), F32), shape((1, 256), F32), shape((1, 256), F32), shape((1024, 128), F32),
        ),
        in_specs=[pl.BlockSpec(memory_space=pl.ANY)] * 3,
        out_specs=(pl.BlockSpec(memory_space=pl.ANY),) + (vmem,) * 7,
        scratch_shapes=[v((32, 8, 128), F32), v((32, 16, 256), BF16), v((1024, 256), BF16), pltpu.SemaphoreType.DMA((4,))],
        compiler_params=pltpu.CompilerParams(vmem_limit_bytes=58 * 1024 * 1024),
        name="lay_out",
    )(ag, sf, wg)
    return (
        ag.reshape(128, 8, 256), lw.T, lbg.reshape(32), rw.T, rbg.reshape(32), gain.reshape(256), shift.reshape(256), ow,
    )


def solution(mesh):
    placed = (P("depth", ("row", "col"), None),) + (P(),) * 9 + (P("row", "col", None),)
    return jax.shard_map(
        body,
        mesh=mesh,
        in_specs=placed,
        out_specs=(P("depth", ("row", "col"), None),) + (P(),) * 7,
        check_vma=False,
    )
```

```python
import functools

import jax
import jax.numpy as jnp
from jax import lax
from jax.experimental import pallas as pl
from jax.experimental.pallas import tpu as pltpu
from jax.sharding import PartitionSpec as P

F32, BF16 = jnp.float32, jnp.bfloat16
MESH = pl.DeviceIdType.MESH
NT = (((1,), (1,)), ((), ()))
TN = (((0,), (0,)), ((), ()))
PAIR, OTHER, LEFT, RIGHT, RSUM, RSUM2, LSUM = range(7)
W1, W2, W3, S1, S2, S3 = range(6)


def dot(a, b):
    return jnp.dot(a, b, preferred_element_type=F32)


def dot_nt(a, b, **kw):
    return lax.dot_general(a, b, NT, preferred_element_type=F32, **kw)


def main_kernel(
    x_any, seq_any, res_any, res_flat, gain_any, shift_any, wl_any, lb_any, wr_any, rb_any, ow_any, pair_any,
    ag_any, sf_any, wg_any,
    pair_ref, x_ref, ow_ref, ag_ref,
    seq_ref, res_ref, res_s, gain_ref, shift_ref, wl_ref, lb_ref, wr_ref, rb_ref, inv1, xf, unit, norm, istd, ngrad, wt, bias, wf, wp, ps, scb, bd, og, outer, lb, lt, rf, rbuf, rt,
    rss, rsr, lss, lsr, lsf, wga, w1s, w1r, w2, w3, wgt, extra, s1s, s1r, s2, s3,
    send_sem, recv_sem, group_send, group_recv, local_sems, load_sems,
):
    depth, row, col = lax.axis_index("depth"), lax.axis_index("row"), lax.axis_index("col")
    z, h = lax.div(row, 2), lax.rem(row, 2)
    q = h * 4 + col
    core = lax.rem(depth, 2)

    moves = (
        (pair_any.at[pl.ds(core * 16, 16)], pair_ref), (seq_any, seq_ref), (res_any, res_ref), (res_flat, res_s),
        (x_any, x_ref), (gain_any, gain_ref), (shift_any, shift_ref), (wl_any, wl_ref), (lb_any, lb_ref),
        (wr_any, wr_ref), (rb_any, rb_ref), (ow_any, ow_ref),
    )
    loads = [pltpu.make_async_copy(src, dst, load_sems.at[n]) for n, (src, dst) in enumerate(moves)]
    for load in loads:
        load.start()

    def zpeer(k):
        t = lax.rem(z + k, 8)
        return t, (depth, t * 2 + h, col)

    def qpeer(k):
        t = lax.rem(q + k, 8)
        return t, (depth, z * 2 + lax.div(t, 4), lax.rem(t, 4))


    g = depth * 8 + q

    def gpeer(k):
        t = lax.rem(g + k, 32)
        u = lax.rem(t, 8)
        return t, (lax.div(t, 8), z * 2 + lax.div(u, 4), lax.rem(u, 4))

    def copy(which, k, src, dst, device):
        return pltpu.make_async_remote_copy(
            src_ref=src, dst_ref=dst, send_sem=send_sem.at[which, k], recv_sem=recv_sem.at[which, k],
            device_id=device, device_id_type=MESH,
        )

    def pair_copy(k):
        t, device = qpeer(k)
        return copy(PAIR, k, ps.at[t], scb.at[core, col, h], device)

    def other_copy(k):
        t = lax.rem(q + 8 - k, 8)
        block = scb.at[core, lax.rem(t, 4), lax.div(t, 4)]
        return copy(OTHER, k, block, block, (depth + 1 - 2 * core, row, col))

    def left_copy(k):
        block = lb.at[pl.ds(pl.multiple_of(q * 256, 256), 256)]
        return copy(LEFT, k, block, block, qpeer(k)[1])

    def right_copy(n):
        to = (1, 7, 2, 6, 7, 1, 6, 2)[n]
        whose = (0, 0, 0, 0, 2, 6, 2, 6)[n]
        block = rbuf.at[lax.rem(z + whose, 8)]
        if n >= 6:
            block = block.at[pl.ds((n - 6) * 128, 128)]
        return copy(RIGHT, n, block, block, zpeer(to)[1])

    def rsum_copy(n, part):
        to = (1, 7, 1, 7, 2, 6)[n]
        whose = (1, 7, 3, 5, 4, 4)[n]
        half = pl.ds(part * 128, 128)
        return copy(RSUM + part, n, rss.at[lax.rem(z + whose, 8), half], rsr.at[n, half], zpeer(to)[1])

    def rsum_late(n, part):
        half = pl.ds(part * 128, 128)
        return copy(RSUM + part, n, rsr.at[n + 2, half], rsr.at[n, half], zpeer((2, 6)[n - 6])[1])

    def rsum_all(part):
        return [functools.partial(rsum_copy, n, part) for n in (2, 3, 4 + part, 0, 1)]

    def lsum_copy(k):
        t, device = qpeer(k)
        return copy(LSUM, k, lss.at[t], lsr.at[k], device)

    def group_copy(which, src, dst, device):
        return pltpu.make_async_remote_copy(
            src_ref=src, dst_ref=dst, send_sem=group_send.at[which], recv_sem=group_recv.at[which],
            device_id=device, device_id_type=MESH,
        )

    def scatter_plane(which, src, dst):
        @pl.loop(1, 32)
        def _(k):
            t, device = gpeer(k)
            group_copy(which, src.at[t], dst.at[k], device).start()

    def share_line(which, ref):
        for k in (4, 3, 5, 2, 6, 1, 7):
            group_copy(which, ref.at[z], ref.at[z], zpeer(k)[1]).start()

    def gather_plane(which, ref):
        @pl.loop(1, 32)
        def _(k):
            group_copy(which, ref.at[g], ref.at[g], gpeer(k)[1]).start()

    def group_wait(which, ref, sems):
        count = ref.shape[0] - 1
        pltpu.make_async_copy(ref.at[pl.ds(1, count)], ref.at[pl.ds(1, count)], sems.at[which]).wait()

    def start(make, count=8):
        for k in range(1, count):
            make(k).start()

    def arrived(make, count=8):
        for k in range(1, count):
            make(k).wait_recv()

    barrier = pltpu.get_barrier_semaphore()
    for k in range(1, 8):
        pl.semaphore_signal(barrier, inc=1, device_id=zpeer(k)[1], device_id_type=MESH)

    @pl.loop(1, 32)
    def _(k):
        pl.semaphore_signal(barrier, inc=1, device_id=gpeer(k)[1], device_id_type=MESH)

    for load in loads[:4]:
        load.wait()
    used = jnp.sum(seq_ref[...].astype(F32), axis=1, keepdims=True)
    res_j = res_ref[:, pl.ds(pl.multiple_of(col * 128, 128), 128)].astype(F32)
    res_j = jnp.broadcast_to(res_j, (128, 128)).T
    inv1[...] = 1.0 / jnp.maximum(used * res_j, 1.0)

    @pl.loop(0, 16, unroll=2)
    def _(i):
        res_i = res_s[row * 32 + core * 16 + i].astype(F32)
        scaled = pair_ref[i].astype(F32) * (inv1[...] * res_i + (1.0 - res_i))
        for t in range(8):
            piece = jnp.concatenate([scaled[t * 8 : t * 8 + 8], scaled[64 + t * 8 : 72 + t * 8]], axis=0)
            ps[t, i] = piece.astype(BF16)

    pl.semaphore_wait(barrier, 38)
    start(pair_copy)
    own_pair = pltpu.make_async_copy(ps.at[q], scb.at[core, col, h], local_sems.at[3])
    own_pair.start()

    for load in loads[4:11]:
        load.wait()
    pick = lax.broadcasted_iota(jnp.int32, (64, 32), 0) - lax.broadcasted_iota(jnp.int32, (64, 32), 1)
    first, second = (pick == 0).astype(F32), (pick == 32).astype(F32)
    wt[0:32, :] = wl_ref[...]
    wt[32:64, :] = wr_ref[...]
    exact = dict(precision=lax.Precision.HIGHEST)
    bias[...] = dot_nt(first, jnp.broadcast_to(lb_ref[...], (128, 32)), **exact) + dot_nt(
        second, jnp.broadcast_to(rb_ref[...], (128, 32)), **exact
    )
    for e in range(2):
        xf[e] = x_ref[:, e * 128 : e * 128 + 128].astype(F32)
    seq_row = seq_ref[:, pl.ds(pl.multiple_of(depth * 128, 128), 128)].astype(F32)
    own_first = (row * 4 + col) * 8

    @pl.loop(0, 8, unroll=4)
    def _(r):
        values = jnp.concatenate([xf[e, pl.ds(r, 128, stride=8), :] for e in range(2)], axis=1)
        centred = values - jnp.mean(values, axis=1, keepdims=True)
        inv_std = lax.rsqrt(jnp.mean(centred * centred, axis=1, keepdims=True) + 1e-05)
        units = centred * inv_std
        normed = (units * gain_ref[...] + shift_ref[...]).astype(BF16)
        unit[r] = units
        norm[r] = normed
        istd[r] = jnp.broadcast_to(inv_std, (128, 128))
        mask = seq_row * res_s[own_first + r].astype(F32)
        both = (dot_nt(wt[...], normed) + bias[...]) * mask
        lb[pl.ds(pl.multiple_of(q * 256 + r * 32, 32), 32), :] = both[:32].astype(BF16)
        rf[pl.ds(r, 32, stride=8), :] = both[32:]

    rbuf[z] = rf[...].astype(BF16)
    for n in (2, 3, 0, 1):
        right_copy(n).start()
    start(left_copy)

    loads[11].wait()
    wf[...] = ow_ref[...].astype(F32)
    for d in range(32):
        wp[d // 2 * 32 : d // 2 * 32 + 32, d % 2 * 128 : d % 2 * 128 + 128] = wf[pl.ds(d, 32, stride=32), :].astype(BF16)

    @pl.loop(0, 64)
    def _(i):
        bd[i] = jnp.zeros((128, 256), BF16)

    own_pair.wait()
    other_copy(0).start()
    for n in (2, 3):
        right_copy(n).wait_recv()
    for n in (4, 5, 6, 7):
        right_copy(n).start()
    for k in range(1, 8):
        pair_copy(k).wait_recv()
        other_copy(k).start()

    def outer_grads(side):
        @pl.loop(0, 16, unroll=8)
        def _(t):
            upper, at = lax.div(t, 8), lax.rem(t, 8) * 2
            i = upper * 32 + side * 16 + at
            for e in range(2):
                block = jnp.concatenate([scb[side, y, upper, at + e] for y in range(4)], axis=0)
                bd[i + e, :64, :128] = block
                bd[i + e, 64:, 128:] = block
            grads = dot_nt(wp[...], bd[pl.ds(i, 2)].reshape(256, 256)).astype(BF16)
            for e in range(2):
                rows = pl.ds(pl.multiple_of((i + e) * 32, 32), 32)
                for p in range(16):
                    og[rows, p * 128 : p * 128 + 128] = grads[p * 32 : p * 32 + 32, e * 128 : e * 128 + 128]

    outer_grads(core)
    for k in range(8):
        other_copy(k).wait_recv()
    outer_grads(1 - core)

    arrived(left_copy)
    for t in range(16):
        block = lb[t * 128 : t * 128 + 128, :].astype(F32)
        lt[:, t * 128 : t * 128 + 128] = block.T.astype(BF16)

    def right_sums(part):
        sums = dot(lt[...], og[:, part * 1024 : part * 1024 + 1024])
        for p in range(8):
            turned = sums[:, p * 128 : p * 128 + 128].T
            at = part * 128 + p * 16
            for t in range(8):
                piece = jnp.concatenate([turned[t * 8 : t * 8 + 8], turned[64 + t * 8 : 72 + t * 8]], axis=0)
                rss[t, at : at + 16, :] = piece.astype(BF16)

    for part in range(2):
        right_sums(part)
        for make in rsum_all(part)[:3]:
            make().start()
    for part in range(2):
        for make in rsum_all(part)[3:]:
            make().start()

    for n in (0, 1, 4, 5, 6, 7):
        right_copy(n).wait_recv()

    @pl.loop(0, 16, unroll=4)
    def _(p):
        blocks = [rbuf[t, pl.ds(pl.multiple_of(p * 16, 16), 16), :].astype(F32) for t in range(8)]
        rows = [block[:8] for block in blocks] + [block[8:] for block in blocks]
        rt[pl.ds(pl.multiple_of(p * 128, 128), 128), :] = jnp.concatenate(rows, axis=0).astype(BF16)

    def left_sum(t):
        at = pl.ds(pl.multiple_of(t * 256, 256), 256)
        lss[t] = dot(og[at, :], rt[...]).astype(BF16)

    def send_left(k):
        left_sum(lax.rem(q + k, 8))
        lsum_copy(k).start()

    def relay(part):
        half = pl.ds(part * 128, 128)
        for make in rsum_all(part)[:3]:
            make().wait_recv()
        for n in range(2):
            total = rss[lax.rem(z + (2, 6)[n], 8), half].astype(F32) + rsr[2 + n, half].astype(F32)
            if n == part:
                total = total + rsr[4 + n, half].astype(F32)
            rsr[8 + n, half] = total.astype(BF16)
            rsum_late(6 + n, part).start()

    @pl.loop(1, 5, unroll=4)
    def _(k):
        send_left(k)

    relay(0)

    @pl.loop(5, 8, unroll=3)
    def _(k):
        send_left(k)

    relay(1)
    left_sum(q)

    @pl.loop(0, 8, unroll=4)
    def _(n):
        at = pl.ds(pl.multiple_of(n * 256, 256), 256)
        for m in range(4):
            product = dot_nt(lb[m * 512 : m * 512 + 512, :], rt[at, :])
            outer[m * 512 : m * 512 + 512, at] = product.astype(BF16)

    wga[...] = jnp.zeros_like(wga)

    @pl.loop(0, 4)
    def _(t):
        blocks = [outer[pl.ds(pl.multiple_of((16 * t + e) * 32, 32), 32), :] for e in range(16)]
        rows = [
            jnp.concatenate([block[:, p * 128 : p * 128 + 128] for block in blocks], axis=1) for p in range(16)
        ]
        wga[...] += dot(jnp.concatenate(rows, axis=0), bd[pl.ds(16 * t, 16)].reshape(2048, 256))

    for t in range(32):
        w1s[t] = wga[t * 16 : t * 16 + 16, :].astype(BF16)
    scatter_plane(W1, w1s, w1r)

    arrived(lsum_copy)
    total = lss[q].astype(F32)
    for k in range(1, 8):
        total = total + lsr[k].astype(F32)
    lsf[...] = total
    for part in range(2):
        for make in rsum_all(part)[3:]:
            make().wait_recv()
    total = rss[z].astype(F32)
    for n in (0, 1, 6, 7):
        if n >= 6:
            rsum_late(n, 0).wait_recv()
            rsum_late(n, 1).wait_recv()
        total = total + rsr[n].astype(F32)
    rf[...] = total

    wgt[...] = jnp.zeros_like(wgt)
    extra[...] = jnp.zeros_like(extra)

    @pl.loop(0, 8, unroll=4)
    def _(r):
        mask = seq_row * res_s[own_first + r].astype(F32)
        sides = [lsf[pl.ds(pl.multiple_of(r * 32, 32), 32), :], rf[pl.ds(r, 32, stride=8), :]]
        pre = (jnp.concatenate(sides, axis=0) * mask).astype(BF16)
        grad = lax.dot_general(pre, wt[...], TN, preferred_element_type=F32)
        ngrad[r] = grad
        wgt[...] += dot(pre, norm[r])
        extra[0:1, :] += jnp.sum(grad * unit[r], axis=0, keepdims=True)
        extra[1:2, :] += jnp.sum(grad, axis=0, keepdims=True)
        extra[2:3, 0:64] += dot_nt(jnp.ones((8, 128), BF16), pre)[0:1]

    upper = lax.broadcasted_iota(jnp.int32, (8, 128), 0) < 4
    for t in range(16):
        tile = wgt[t // 2 * 8 : t // 2 * 8 + 8, t % 2 * 128 : t % 2 * 128 + 128]
        s1s[2 * t] = jnp.where(upper, tile, 0.0)
        s1s[2 * t + 1] = jnp.where(upper, 0.0, tile)
    s1s[0, 4:5, :] = extra[0:1, :128]
    s1s[1, 0:1, :] = extra[0:1, 128:]
    s1s[2, 4:5, :] = extra[1:2, :128]
    s1s[3, 0:1, :] = extra[1:2, 128:]
    s1s[4, 4:5, :] = extra[2:3, :128]
    scatter_plane(S1, s1s, s1r)

    def input_grad(r):
        units = unit[r]
        weighted = ngrad[r] * gain_ref[...]
        mean = jnp.mean(weighted, axis=1, keepdims=True)
        along = jnp.mean(weighted * units, axis=1, keepdims=True)
        scale = jnp.concatenate([istd[r], istd[r]], axis=1)
        result = scale * (weighted - mean - units * along)
        for e in range(2):
            xf[e, pl.ds(r, 128, stride=8), :] = result[:, e * 128 : e * 128 + 128]

    def summed(ref, count, first):
        total = first
        for k in range(1, count):
            total = total + ref[k].astype(F32)
        return total

    @pl.loop(0, 4, unroll=4)
    def _(r):
        input_grad(r)

    group_wait(W1, w1r, group_recv)
    w2[z] = summed(w1r, 32, wga[pl.ds(pl.multiple_of(g * 16, 16), 16), :]).astype(BF16)
    share_line(W2, w2)
    group_wait(S1, s1r, group_recv)
    s2[z] = summed(s1r, 32, s1s[g])
    share_line(S2, s2)

    @pl.loop(4, 8, unroll=4)
    def _(r):
        input_grad(r)

    for e in range(2):
        ag_ref[:, e * 128 : e * 128 + 128] = xf[e].astype(BF16)
    store = pltpu.make_async_copy(ag_ref, ag_any, local_sems.at[4])
    store.start()

    group_wait(W2, w2, group_recv)
    w3[g] = summed(w2, 8, w2[0].astype(F32)).astype(BF16)
    gather_plane(W3, w3)
    group_wait(S2, s2, group_recv)
    s3[g] = summed(s2, 8, s2[0])
    gather_plane(S3, s3)

    for make in (pair_copy, left_copy, lsum_copy):
        for k in range(1, 8):
            make(k).wait_send()
    for n in range(8):
        other_copy(n).wait_send()
        right_copy(n).wait_send()
    for make in rsum_all(0) + rsum_all(1):
        make().wait_send()
    for n in (6, 7):
        rsum_late(n, 0).wait_send()
        rsum_late(n, 1).wait_send()
    for which, ref in ((W1, w1s), (W2, w2), (W3, w3), (S1, s1s), (S2, s2), (S3, s3)):
        group_wait(which, ref, group_send)

    group_wait(W3, w3, group_recv)
    store_wg = pltpu.make_async_copy(w3, wg_any, local_sems.at[0])
    store_wg.start()
    group_wait(S3, s3, group_recv)
    store_sf = pltpu.make_async_copy(s3, sf_any, local_sems.at[1])
    store_sf.start()
    store.wait()
    store_wg.wait()
    store_sf.wait()


def last_kernel(
    ag_any, sf_any, wg_any, ag_out, lw_ref, lb_ref, rw_ref, rb_ref, gain_ref, shift_ref, ow_ref, sf, wg, ag, sems
):
    moves = [
        pltpu.make_async_copy(src, dst, sems.at[n])
        for n, (src, dst) in enumerate(((ag_any, ag), (wg_any, wg), (sf_any, sf), (ag, ag_out)))
    ]
    for move in moves[:3]:
        move.start()
    moves[0].wait()
    moves[3].start()
    moves[1].wait()
    for d in range(32):
        tile = wg[d // 2 * 2 : d // 2 * 2 + 2, :, d % 2 * 128 : d % 2 * 128 + 128].reshape(32, 128)
        ow_ref[pl.ds(d, 32, stride=32), :] = tile.astype(F32)
    moves[2].wait()
    upper = lax.broadcasted_iota(jnp.int32, (8, 128), 0) < 4
    for t in range(16):
        tile = jnp.where(upper, sf[2 * t], sf[2 * t + 1])
        side, row, lane = (lw_ref, rw_ref)[t // 8], t % 8 // 2 * 8, t % 2 * 128
        side[row : row + 8, lane : lane + 128] = tile
    gain_ref[:, :128] = sf[0, 4:5, :]
    gain_ref[:, 128:] = sf[1, 0:1, :]
    shift_ref[:, :128] = sf[2, 4:5, :]
    shift_ref[:, 128:] = sf[3, 0:1, :]
    lb_ref[...] = sf[4, 4:5, 0:32]
    rb_ref[...] = sf[4, 4:5, 32:64]
    moves[3].wait()


def body(
    alignment, seq_mask, residue_mask, layer_norm_gain, layer_norm_bias, left_projection_weight, left_bias,
    right_projection_weight, right_bias, out_weight, pair_grad,
):
    vmem = pl.BlockSpec(memory_space=pltpu.VMEM)
    hbm = pl.BlockSpec(memory_space=pl.ANY)
    v = pltpu.VMEM
    shape = jax.ShapeDtypeStruct
    scratch = [
        v((16, 128, 128), BF16),
        v((1024, 256), BF16),
        v((1024, 128), BF16),
        v((1024, 256), BF16),
        v((1, 512), jnp.int32),
        v((1, 512), jnp.int32),
        pltpu.SMEM((512,), jnp.int32),
        v((1, 256), F32),
        v((1, 256), F32),
        v((32, 256), BF16),
        v((1, 32), F32),
        v((32, 256), BF16),
        v((1, 32), F32),
        v((128, 128), F32),
        v((2, 1024, 128), F32),
        v((8, 128, 256), F32),
        v((8, 128, 256), BF16),
        v((8, 128, 128), F32),
        v((8, 128, 256), F32),
        v((64, 256), BF16),
        v((64, 128), F32),
        v((1024, 128), F32),
        v((512, 256), BF16),
        v((8, 16, 16, 128), BF16),
        v((2, 4, 2, 16, 16, 128), BF16),
        v((64, 128, 256), BF16),
        v((2048, 2048), BF16),
        v((2048, 2048), BF16),
        v((2048, 128), BF16),
        v((128, 2048), BF16),
        v((256, 128), F32),
        v((8, 256, 128), BF16),
        v((2048, 128), BF16),
        v((8, 256, 128), BF16),
        v((10, 256, 128), BF16),
        v((8, 256, 128), BF16),
        v((8, 256, 128), BF16),
        v((256, 128), F32),
        v((512, 256), F32),
        v((32, 16, 256), BF16),
        v((32, 16, 256), BF16),
        v((8, 16, 256), BF16),
        v((32, 16, 256), BF16),
        v((64, 256), F32),
        v((8, 256), F32),
        v((32, 8, 128), F32),
        v((32, 8, 128), F32),
        v((8, 8, 128), F32),
        v((32, 8, 128), F32),
        pltpu.SemaphoreType.DMA((7, 8)),
        pltpu.SemaphoreType.DMA((7, 8)),
        pltpu.SemaphoreType.DMA((6,)),
        pltpu.SemaphoreType.DMA((6,)),
        pltpu.SemaphoreType.DMA((5,)),
        pltpu.SemaphoreType.DMA((12,)),
    ]
    ag, sf, wg = pl.pallas_call(
        main_kernel,
        out_shape=(shape((1024, 256), BF16), shape((32, 8, 128), F32), shape((32, 16, 256), BF16)),
        in_specs=[hbm] * 12,
        out_specs=(hbm,) * 3,
        scratch_shapes=scratch,
        compiler_params=pltpu.CompilerParams(
            collective_id=0, has_side_effects=True, vmem_limit_bytes=58 * 1024 * 1024
        ),
        name="pair_backward",
    )(
        alignment.reshape(1024, 256), seq_mask.reshape(1, 512), residue_mask.reshape(1, 512), residue_mask,
        layer_norm_gain.reshape(1, 256), layer_norm_bias.reshape(1, 256), left_projection_weight.T,
        left_bias.reshape(1, 32), right_projection_weight.T, right_bias.reshape(1, 32), out_weight, pair_grad,
    )
    ag, lw, lbg, rw, rbg, gain, shift, ow = pl.pallas_call(
        last_kernel,
        out_shape=(
            shape((1024, 256), BF16), shape((32, 256), F32), shape((1, 32), F32), shape((32, 256), F32),
            shape((1, 32), F32), shape((1, 256), F32), shape((1, 256), F32), shape((1024, 128), F32),
        ),
        in_specs=[pl.BlockSpec(memory_space=pl.ANY)] * 3,
        out_specs=(pl.BlockSpec(memory_space=pl.ANY),) + (vmem,) * 7,
        scratch_shapes=[v((32, 8, 128), F32), v((32, 16, 256), BF16), v((1024, 256), BF16), pltpu.SemaphoreType.DMA((4,))],
        compiler_params=pltpu.CompilerParams(vmem_limit_bytes=58 * 1024 * 1024),
        name="lay_out",
    )(ag, sf, wg)
    return (
        ag.reshape(128, 8, 256), lw.T, lbg.reshape(32), rw.T, rbg.reshape(32), gain.reshape(256), shift.reshape(256), ow,
    )


def solution(mesh):
    placed = (P("depth", ("row", "col"), None),) + (P(),) * 9 + (P("row", "col", None),)
    return jax.shard_map(
        body,
        mesh=mesh,
        in_specs=placed,
        out_specs=(P("depth", ("row", "col"), None),) + (P(),) * 7,
        check_vma=False,
    )
```

```python
import jax
import jax.numpy as jnp
from jax import lax
from jax.experimental import pallas as pl
from jax.experimental.pallas import tpu as pltpu
from jax.sharding import PartitionSpec as P

F32, BF16 = jnp.float32, jnp.bfloat16
MESH = pl.DeviceIdType.MESH
NT = (((1,), (1,)), ((), ()))
TN = (((0,), (0,)), ((), ()))
PAIR, OTHER, LEFT, RIGHT, RSUM, RSUM2, LSUM = range(7)
W1, W2, W3, S1, S2, S3 = range(6)


def dot(a, b):
    return jnp.dot(a, b, preferred_element_type=F32)


def dot_nt(a, b, **kw):
    return lax.dot_general(a, b, NT, preferred_element_type=F32, **kw)


def main_kernel(
    x_any, seq_any, res_any, res_flat, gain_any, shift_any, wl_any, lb_any, wr_any, rb_any, ow_any, pair_any,
    ag_any, sf_any, wg_any,
    pair_ref, x_ref, ow_ref, ag_ref,
    seq_ref, res_ref, res_s, gain_ref, shift_ref, wl_ref, lb_ref, wr_ref, rb_ref, inv1, xf, unit, norm, istd, ngrad, wt, bias, wf, wp, ps, scb, bd, og, outer, lb, lt, rf, rbuf, rt,
    rss, rsr, lss, lsr, lsf, wga, w1s, w1r, w2, w3, wgt, extra, s1s, s1r, s2, s3,
    send_sem, recv_sem, group_send, group_recv, local_sems, load_sems,
):
    depth, row, col = lax.axis_index("depth"), lax.axis_index("row"), lax.axis_index("col")
    z, h = lax.div(row, 2), lax.rem(row, 2)
    q = h * 4 + col
    core = lax.rem(depth, 2)

    moves = (
        (pair_any.at[pl.ds(core * 16, 16)], pair_ref), (seq_any, seq_ref), (res_any, res_ref), (res_flat, res_s),
        (x_any, x_ref), (gain_any, gain_ref), (shift_any, shift_ref), (wl_any, wl_ref), (lb_any, lb_ref),
        (wr_any, wr_ref), (rb_any, rb_ref), (ow_any, ow_ref),
    )
    loads = [pltpu.make_async_copy(src, dst, load_sems.at[n]) for n, (src, dst) in enumerate(moves)]
    for load in loads:
        load.start()

    def zpeer(k):
        t = lax.rem(z + k, 8)
        return t, (depth, t * 2 + h, col)

    def qpeer(k):
        t = lax.rem(q + k, 8)
        return t, (depth, z * 2 + lax.div(t, 4), lax.rem(t, 4))

    g = depth * 8 + q

    def gpeer(k):
        t = lax.rem(g + k, 32)
        u = lax.rem(t, 8)
        return t, (lax.div(t, 8), z * 2 + lax.div(u, 4), lax.rem(u, 4))

    def copy(which, k, src, dst, device):
        return pltpu.make_async_remote_copy(
            src_ref=src, dst_ref=dst, send_sem=send_sem.at[which, k], recv_sem=recv_sem.at[which, k],
            device_id=device, device_id_type=MESH,
        )

    def pair_copy(k):
        t, device = qpeer(k)
        return copy(PAIR, k, ps.at[t], scb.at[core, col, h], device)

    def other_copy(k):
        t = lax.rem(q + 8 - k, 8)
        block = scb.at[core, lax.rem(t, 4), lax.div(t, 4)]
        return copy(OTHER, k, block, block, (depth + 1 - 2 * core, row, col))

    def left_copy(k):
        block = lb.at[pl.ds(pl.multiple_of(q * 256, 256), 256)]
        return copy(LEFT, k, block, block, qpeer(k)[1])

    def right_copy(k):
        return copy(RIGHT, k, rbuf.at[z], rbuf.at[z], zpeer(k)[1])

    def rsum_copy(k, part):
        t, device = zpeer(k)
        half = pl.ds(part * 128, 128)
        return copy(RSUM + part, k, rss.at[t, half], rsr.at[k, half], device)

    def lsum_copy(k):
        t, device = qpeer(k)
        return copy(LSUM, k, lss.at[t], lsr.at[k], device)

    def group_copy(which, src, dst, device):
        return pltpu.make_async_remote_copy(
            src_ref=src, dst_ref=dst, send_sem=group_send.at[which], recv_sem=group_recv.at[which],
            device_id=device, device_id_type=MESH,
        )

    def scatter_plane(which, src, dst):
        @pl.loop(1, 32)
        def _(k):
            t, device = gpeer(k)
            group_copy(which, src.at[t], dst.at[k], device).start()

    def share_line(which, ref):
        for k in (4, 3, 5, 2, 6, 1, 7):
            group_copy(which, ref.at[z], ref.at[z], zpeer(k)[1]).start()

    def gather_plane(which, ref):
        @pl.loop(1, 32)
        def _(k):
            group_copy(which, ref.at[g], ref.at[g], gpeer(k)[1]).start()

    def group_wait(which, ref, sems):
        count = ref.shape[0] - 1
        pltpu.make_async_copy(ref.at[pl.ds(1, count)], ref.at[pl.ds(1, count)], sems.at[which]).wait()

    def start(make, count=8):
        for k in range(1, count):
            make(k).start()

    def arrived(make, count=8):
        for k in range(1, count):
            make(k).wait_recv()

    barrier = pltpu.get_barrier_semaphore()
    for k in range(1, 8):
        pl.semaphore_signal(barrier, inc=1, device_id=zpeer(k)[1], device_id_type=MESH)

    @pl.loop(1, 32)
    def _(k):
        pl.semaphore_signal(barrier, inc=1, device_id=gpeer(k)[1], device_id_type=MESH)

    for load in loads[:4]:
        load.wait()
    used = jnp.sum(seq_ref[...].astype(F32), axis=1, keepdims=True)
    res_j = res_ref[:, pl.ds(pl.multiple_of(col * 128, 128), 128)].astype(F32)
    res_j = jnp.broadcast_to(res_j, (128, 128)).T
    inv1[...] = 1.0 / jnp.maximum(used * res_j, 1.0)

    @pl.loop(0, 16, unroll=2)
    def _(i):
        res_i = res_s[row * 32 + core * 16 + i].astype(F32)
        scaled = pair_ref[i].astype(F32) * (inv1[...] * res_i + (1.0 - res_i))
        for t in range(8):
            piece = jnp.concatenate([scaled[t * 8 : t * 8 + 8], scaled[64 + t * 8 : 72 + t * 8]], axis=0)
            ps[t, i] = piece.astype(BF16)

    pl.semaphore_wait(barrier, 38)
    start(pair_copy)
    own_pair = pltpu.make_async_copy(ps.at[q], scb.at[core, col, h], local_sems.at[3])
    own_pair.start()

    for load in loads[4:11]:
        load.wait()
    pick = lax.broadcasted_iota(jnp.int32, (64, 32), 0) - lax.broadcasted_iota(jnp.int32, (64, 32), 1)
    first, second = (pick == 0).astype(F32), (pick == 32).astype(F32)
    wt[0:32, :] = wl_ref[...]
    wt[32:64, :] = wr_ref[...]
    exact = dict(precision=lax.Precision.HIGHEST)
    bias[...] = dot_nt(first, jnp.broadcast_to(lb_ref[...], (128, 32)), **exact) + dot_nt(
        second, jnp.broadcast_to(rb_ref[...], (128, 32)), **exact
    )
    for e in range(2):
        xf[e] = x_ref[:, e * 128 : e * 128 + 128].astype(F32)
    seq_row = seq_ref[:, pl.ds(pl.multiple_of(depth * 128, 128), 128)].astype(F32)
    own_first = (row * 4 + col) * 8

    @pl.loop(0, 8, unroll=4)
    def _(r):
        values = jnp.concatenate([xf[e, pl.ds(r, 128, stride=8), :] for e in range(2)], axis=1)
        centred = values - jnp.mean(values, axis=1, keepdims=True)
        inv_std = lax.rsqrt(jnp.mean(centred * centred, axis=1, keepdims=True) + 1e-05)
        units = centred * inv_std
        normed = (units * gain_ref[...] + shift_ref[...]).astype(BF16)
        unit[r] = units
        norm[r] = normed
        istd[r] = jnp.broadcast_to(inv_std, (128, 128))
        mask = seq_row * res_s[own_first + r].astype(F32)
        both = (dot_nt(wt[...], normed) + bias[...]) * mask
        lb[pl.ds(pl.multiple_of(q * 256 + r * 32, 32), 32), :] = both[:32].astype(BF16)
        rf[pl.ds(r, 32, stride=8), :] = both[32:]

    rbuf[z] = rf[...].astype(BF16)
    start(left_copy)
    for k in (4, 3, 5, 2, 6, 1, 7):
        right_copy(k).start()

    loads[11].wait()
    wf[...] = ow_ref[...].astype(F32)
    for d in range(32):
        wp[d // 2 * 32 : d // 2 * 32 + 32, d % 2 * 128 : d % 2 * 128 + 128] = wf[pl.ds(d, 32, stride=32), :].astype(BF16)

    @pl.loop(0, 64)
    def _(i):
        bd[i] = jnp.zeros((128, 256), BF16)

    own_pair.wait()
    other_copy(0).start()
    for k in range(1, 8):
        pair_copy(k).wait_recv()
        other_copy(k).start()

    def outer_grads(side):
        @pl.loop(0, 16, unroll=8)
        def _(t):
            upper, at = lax.div(t, 8), lax.rem(t, 8) * 2
            i = upper * 32 + side * 16 + at
            for e in range(2):
                block = jnp.concatenate([scb[side, y, upper, at + e] for y in range(4)], axis=0)
                bd[i + e, :64, :128] = block
                bd[i + e, 64:, 128:] = block
            grads = dot_nt(wp[...], bd[pl.ds(i, 2)].reshape(256, 256)).astype(BF16)
            for e in range(2):
                rows = pl.ds(pl.multiple_of((i + e) * 32, 32), 32)
                for p in range(16):
                    og[rows, p * 128 : p * 128 + 128] = grads[p * 32 : p * 32 + 32, e * 128 : e * 128 + 128]

    outer_grads(core)
    for k in range(8):
        other_copy(k).wait_recv()
    outer_grads(1 - core)

    arrived(left_copy)
    for t in range(16):
        block = lb[t * 128 : t * 128 + 128, :].astype(F32)
        lt[:, t * 128 : t * 128 + 128] = block.T.astype(BF16)

    def right_sums(part):
        sums = dot(lt[...], og[:, part * 1024 : part * 1024 + 1024])
        for p in range(8):
            turned = sums[:, p * 128 : p * 128 + 128].T
            at = part * 128 + p * 16
            for t in range(8):
                piece = jnp.concatenate([turned[t * 8 : t * 8 + 8], turned[64 + t * 8 : 72 + t * 8]], axis=0)
                rss[t, at : at + 16, :] = piece.astype(BF16)

    for part in range(2):
        right_sums(part)
        for k in (4, 3, 5, 2, 6, 1, 7):
            rsum_copy(k, part).start()

    arrived(right_copy)

    @pl.loop(0, 16, unroll=4)
    def _(p):
        blocks = [rbuf[t, pl.ds(pl.multiple_of(p * 16, 16), 16), :].astype(F32) for t in range(8)]
        rows = [block[:8] for block in blocks] + [block[8:] for block in blocks]
        rt[pl.ds(pl.multiple_of(p * 128, 128), 128), :] = jnp.concatenate(rows, axis=0).astype(BF16)

    def left_sum(t):
        at = pl.ds(pl.multiple_of(t * 256, 256), 256)
        lss[t] = dot(og[at, :], rt[...]).astype(BF16)

    def send_left(k):
        left_sum(lax.rem(q + k, 8))
        lsum_copy(k).start()

    @pl.loop(1, 8)
    def _(k):
        send_left(k)

    left_sum(q)

    @pl.loop(0, 8, unroll=4)
    def _(n):
        at = pl.ds(pl.multiple_of(n * 256, 256), 256)
        for m in range(4):
            product = dot_nt(lb[m * 512 : m * 512 + 512, :], rt[at, :])
            outer[m * 512 : m * 512 + 512, at] = product.astype(BF16)

    wga[...] = jnp.zeros_like(wga)

    @pl.loop(0, 4)
    def _(t):
        blocks = [outer[pl.ds(pl.multiple_of((16 * t + e) * 32, 32), 32), :] for e in range(16)]
        rows = [
            jnp.concatenate([block[:, p * 128 : p * 128 + 128] for block in blocks], axis=1) for p in range(16)
        ]
        wga[...] += dot(jnp.concatenate(rows, axis=0), bd[pl.ds(16 * t, 16)].reshape(2048, 256))

    for t in range(32):
        w1s[t] = wga[t * 16 : t * 16 + 16, :].astype(BF16)
    scatter_plane(W1, w1s, w1r)

    arrived(lsum_copy)
    total = lss[q].astype(F32)
    for k in range(1, 8):
        total = total + lsr[k].astype(F32)
    lsf[...] = total
    total = rss[z].astype(F32)
    for k in range(1, 8):
        rsum_copy(k, 0).wait_recv()
        rsum_copy(k, 1).wait_recv()
        total = total + rsr[k].astype(F32)
    rf[...] = total

    wgt[...] = jnp.zeros_like(wgt)
    extra[...] = jnp.zeros_like(extra)

    @pl.loop(0, 8, unroll=4)
    def _(r):
        mask = seq_row * res_s[own_first + r].astype(F32)
        sides = [lsf[pl.ds(pl.multiple_of(r * 32, 32), 32), :], rf[pl.ds(r, 32, stride=8), :]]
        pre = (jnp.concatenate(sides, axis=0) * mask).astype(BF16)
        grad = lax.dot_general(pre, wt[...], TN, preferred_element_type=F32)
        ngrad[r] = grad
        wgt[...] += dot(pre, norm[r])
        extra[0:1, :] += jnp.sum(grad * unit[r], axis=0, keepdims=True)
        extra[1:2, :] += jnp.sum(grad, axis=0, keepdims=True)
        extra[2:3, 0:64] += dot_nt(jnp.ones((8, 128), BF16), pre)[0:1]

    upper = lax.broadcasted_iota(jnp.int32, (8, 128), 0) < 4
    for t in range(16):
        tile = wgt[t // 2 * 8 : t // 2 * 8 + 8, t % 2 * 128 : t % 2 * 128 + 128]
        s1s[2 * t] = jnp.where(upper, tile, 0.0)
        s1s[2 * t + 1] = jnp.where(upper, 0.0, tile)
    s1s[0, 4:5, :] = extra[0:1, :128]
    s1s[1, 0:1, :] = extra[0:1, 128:]
    s1s[2, 4:5, :] = extra[1:2, :128]
    s1s[3, 0:1, :] = extra[1:2, 128:]
    s1s[4, 4:5, :] = extra[2:3, :128]
    scatter_plane(S1, s1s, s1r)

    def input_grad(r):
        units = unit[r]
        weighted = ngrad[r] * gain_ref[...]
        mean = jnp.mean(weighted, axis=1, keepdims=True)
        along = jnp.mean(weighted * units, axis=1, keepdims=True)
        scale = jnp.concatenate([istd[r], istd[r]], axis=1)
        result = scale * (weighted - mean - units * along)
        for e in range(2):
            xf[e, pl.ds(r, 128, stride=8), :] = result[:, e * 128 : e * 128 + 128]

    def summed(ref, count, first):
        total = first
        for k in range(1, count):
            total = total + ref[k].astype(F32)
        return total

    @pl.loop(0, 4, unroll=4)
    def _(r):
        input_grad(r)

    group_wait(W1, w1r, group_recv)
    w2[z] = summed(w1r, 32, wga[pl.ds(pl.multiple_of(g * 16, 16), 16), :]).astype(BF16)
    share_line(W2, w2)
    group_wait(S1, s1r, group_recv)
    s2[z] = summed(s1r, 32, s1s[g])
    share_line(S2, s2)

    @pl.loop(4, 8, unroll=4)
    def _(r):
        input_grad(r)

    for e in range(2):
        ag_ref[:, e * 128 : e * 128 + 128] = xf[e].astype(BF16)
    store = pltpu.make_async_copy(ag_ref, ag_any, local_sems.at[4])
    store.start()

    group_wait(W2, w2, group_recv)
    w3[g] = summed(w2, 8, w2[0].astype(F32)).astype(BF16)
    gather_plane(W3, w3)
    group_wait(S2, s2, group_recv)
    s3[g] = summed(s2, 8, s2[0])
    gather_plane(S3, s3)

    for make in (pair_copy, left_copy, lsum_copy):
        for k in range(1, 8):
            make(k).wait_send()
    for n in range(8):
        other_copy(n).wait_send()
    for k in range(1, 8):
        right_copy(k).wait_send()
    for k in range(1, 8):
        rsum_copy(k, 0).wait_send()
        rsum_copy(k, 1).wait_send()
    for which, ref in ((W1, w1s), (W2, w2), (W3, w3), (S1, s1s), (S2, s2), (S3, s3)):
        group_wait(which, ref, group_send)

    group_wait(W3, w3, group_recv)
    store_wg = pltpu.make_async_copy(w3, wg_any, local_sems.at[0])
    store_wg.start()
    group_wait(S3, s3, group_recv)
    store_sf = pltpu.make_async_copy(s3, sf_any, local_sems.at[1])
    store_sf.start()
    store.wait()
    store_wg.wait()
    store_sf.wait()


def last_kernel(
    ag_any, sf_any, wg_any, ag_out, lw_ref, lb_ref, rw_ref, rb_ref, gain_ref, shift_ref, ow_ref, sf, wg, ag, sems
):
    moves = [
        pltpu.make_async_copy(src, dst, sems.at[n])
        for n, (src, dst) in enumerate(((ag_any, ag), (wg_any, wg), (sf_any, sf), (ag, ag_out)))
    ]
    for move in moves[:3]:
        move.start()
    moves[0].wait()
    moves[3].start()
    moves[1].wait()
    for d in range(32):
        tile = wg[d // 2 * 2 : d // 2 * 2 + 2, :, d % 2 * 128 : d % 2 * 128 + 128].reshape(32, 128)
        ow_ref[pl.ds(d, 32, stride=32), :] = tile.astype(F32)
    moves[2].wait()
    upper = lax.broadcasted_iota(jnp.int32, (8, 128), 0) < 4
    for t in range(16):
        tile = jnp.where(upper, sf[2 * t], sf[2 * t + 1])
        side, row, lane = (lw_ref, rw_ref)[t // 8], t % 8 // 2 * 8, t % 2 * 128
        side[row : row + 8, lane : lane + 128] = tile
    gain_ref[:, :128] = sf[0, 4:5, :]
    gain_ref[:, 128:] = sf[1, 0:1, :]
    shift_ref[:, :128] = sf[2, 4:5, :]
    shift_ref[:, 128:] = sf[3, 0:1, :]
    lb_ref[...] = sf[4, 4:5, 0:32]
    rb_ref[...] = sf[4, 4:5, 32:64]
    moves[3].wait()


def body(
    alignment, seq_mask, residue_mask, layer_norm_gain, layer_norm_bias, left_projection_weight, left_bias,
    right_projection_weight, right_bias, out_weight, pair_grad,
):
    vmem = pl.BlockSpec(memory_space=pltpu.VMEM)
    hbm = pl.BlockSpec(memory_space=pl.ANY)
    v = pltpu.VMEM
    shape = jax.ShapeDtypeStruct
    scratch = [
        v((16, 128, 128), BF16),
        v((1024, 256), BF16),
        v((1024, 128), BF16),
        v((1024, 256), BF16),
        v((1, 512), jnp.int32),
        v((1, 512), jnp.int32),
        pltpu.SMEM((512,), jnp.int32),
        v((1, 256), F32),
        v((1, 256), F32),
        v((32, 256), BF16),
        v((1, 32), F32),
        v((32, 256), BF16),
        v((1, 32), F32),
        v((128, 128), F32),
        v((2, 1024, 128), F32),
        v((8, 128, 256), F32),
        v((8, 128, 256), BF16),
        v((8, 128, 128), F32),
        v((8, 128, 256), F32),
        v((64, 256), BF16),
        v((64, 128), F32),
        v((1024, 128), F32),
        v((512, 256), BF16),
        v((8, 16, 16, 128), BF16),
        v((2, 4, 2, 16, 16, 128), BF16),
        v((64, 128, 256), BF16),
        v((2048, 2048), BF16),
        v((2048, 2048), BF16),
        v((2048, 128), BF16),
        v((128, 2048), BF16),
        v((256, 128), F32),
        v((8, 256, 128), BF16),
        v((2048, 128), BF16),
        v((8, 256, 128), BF16),
        v((8, 256, 128), BF16),
        v((8, 256, 128), BF16),
        v((8, 256, 128), BF16),
        v((256, 128), F32),
        v((512, 256), F32),
        v((32, 16, 256), BF16),
        v((32, 16, 256), BF16),
        v((8, 16, 256), BF16),
        v((32, 16, 256), BF16),
        v((64, 256), F32),
        v((8, 256), F32),
        v((32, 8, 128), F32),
        v((32, 8, 128), F32),
        v((8, 8, 128), F32),
        v((32, 8, 128), F32),
        pltpu.SemaphoreType.DMA((7, 8)),
        pltpu.SemaphoreType.DMA((7, 8)),
        pltpu.SemaphoreType.DMA((6,)),
        pltpu.SemaphoreType.DMA((6,)),
        pltpu.SemaphoreType.DMA((5,)),
        pltpu.SemaphoreType.DMA((12,)),
    ]
    ag, sf, wg = pl.pallas_call(
        main_kernel,
        out_shape=(shape((1024, 256), BF16), shape((32, 8, 128), F32), shape((32, 16, 256), BF16)),
        in_specs=[hbm] * 12,
        out_specs=(hbm,) * 3,
        scratch_shapes=scratch,
        compiler_params=pltpu.CompilerParams(
            collective_id=0, has_side_effects=True, vmem_limit_bytes=58 * 1024 * 1024
        ),
        name="pair_backward",
    )(
        alignment.reshape(1024, 256), seq_mask.reshape(1, 512), residue_mask.reshape(1, 512), residue_mask,
        layer_norm_gain.reshape(1, 256), layer_norm_bias.reshape(1, 256), left_projection_weight.T,
        left_bias.reshape(1, 32), right_projection_weight.T, right_bias.reshape(1, 32), out_weight, pair_grad,
    )
    ag, lw, lbg, rw, rbg, gain, shift, ow = pl.pallas_call(
        last_kernel,
        out_shape=(
            shape((1024, 256), BF16), shape((32, 256), F32), shape((1, 32), F32), shape((32, 256), F32),
            shape((1, 32), F32), shape((1, 256), F32), shape((1, 256), F32), shape((1024, 128), F32),
        ),
        in_specs=[pl.BlockSpec(memory_space=pl.ANY)] * 3,
        out_specs=(pl.BlockSpec(memory_space=pl.ANY),) + (vmem,) * 7,
        scratch_shapes=[v((32, 8, 128), F32), v((32, 16, 256), BF16), v((1024, 256), BF16), pltpu.SemaphoreType.DMA((4,))],
        compiler_params=pltpu.CompilerParams(vmem_limit_bytes=58 * 1024 * 1024),
        name="lay_out",
    )(ag, sf, wg)
    return (
        ag.reshape(128, 8, 256), lw.T, lbg.reshape(32), rw.T, rbg.reshape(32), gain.reshape(256), shift.reshape(256), ow,
    )


def solution(mesh):
    placed = (P("depth", ("row", "col"), None),) + (P(),) * 9 + (P("row", "col", None),)
    return jax.shard_map(
        body,
        mesh=mesh,
        in_specs=placed,
        out_specs=(P("depth", ("row", "col"), None),) + (P(),) * 7,
        check_vma=False,
    )
```

```python
import jax
import jax.numpy as jnp
from jax import lax
from jax.experimental import pallas as pl
from jax.experimental.pallas import tpu as pltpu
from jax.sharding import PartitionSpec as P

F32, BF16 = jnp.float32, jnp.bfloat16
MESH = pl.DeviceIdType.MESH
NT = (((1,), (1,)), ((), ()))
TN = (((0,), (0,)), ((), ()))
PAIR, OTHER, LEFT, RIGHT, RSUM, RSUM2, LSUM = range(7)
W1, W2, W3, S1, S2, S3 = range(6)


def dot(a, b):
    return jnp.dot(a, b, preferred_element_type=F32)


def dot_nt(a, b, **kw):
    return lax.dot_general(a, b, NT, preferred_element_type=F32, **kw)


def main_kernel(
    x_any, seq_any, res_any, res_flat, gain_any, shift_any, wl_any, lb_any, wr_any, rb_any, ow_any, pair_any,
    ag_any, sf_any, wg_any,
    pair_ref, x_ref, ow_ref, ag_ref,
    seq_ref, res_ref, res_s, gain_ref, shift_ref, wl_ref, lb_ref, wr_ref, rb_ref, inv1, xf, unit, norm, istd, ngrad, wt, bias, wf, wp, ps, scb, bd, og, outer, lb, lt, rf, rbuf, rt,
    rss, rsr, lss, lsr, lsf, wga, w1s, w1r, w2, w3, wgt, extra, s1s, s1r, s2, s3,
    send_sem, recv_sem, group_send, group_recv, local_sems, load_sems,
):
    depth, row, col = lax.axis_index("depth"), lax.axis_index("row"), lax.axis_index("col")
    z, h = lax.div(row, 2), lax.rem(row, 2)
    q = h * 4 + col
    core = lax.rem(depth, 2)

    moves = (
        (pair_any.at[pl.ds(core * 16, 16)], pair_ref), (seq_any, seq_ref), (res_any, res_ref), (res_flat, res_s),
        (x_any, x_ref), (gain_any, gain_ref), (shift_any, shift_ref), (wl_any, wl_ref), (lb_any, lb_ref),
        (wr_any, wr_ref), (rb_any, rb_ref), (ow_any, ow_ref),
    )
    loads = [pltpu.make_async_copy(src, dst, load_sems.at[n]) for n, (src, dst) in enumerate(moves)]
    for load in loads:
        load.start()

    def zpeer(k):
        t = lax.rem(z + k, 8)
        return t, (depth, t * 2 + h, col)

    def qpeer(k):
        t = lax.rem(q + k, 8)
        return t, (depth, z * 2 + lax.div(t, 4), lax.rem(t, 4))

    g = depth * 8 + q

    def gpeer(k):
        t = lax.rem(g + k, 32)
        u = lax.rem(t, 8)
        return t, (lax.div(t, 8), z * 2 + lax.div(u, 4), lax.rem(u, 4))

    def copy(which, k, src, dst, device):
        return pltpu.make_async_remote_copy(
            src_ref=src, dst_ref=dst, send_sem=send_sem.at[which, k], recv_sem=recv_sem.at[which, k],
            device_id=device, device_id_type=MESH,
        )

    def pair_copy(k):
        t, device = qpeer(k)
        return copy(PAIR, k, ps.at[t], scb.at[core, col, h], device)

    def other_copy(k):
        t = lax.rem(q + 8 - k, 8)
        block = scb.at[core, lax.rem(t, 4), lax.div(t, 4)]
        return copy(OTHER, k, block, block, (depth + 1 - 2 * core, row, col))

    def left_copy(k):
        block = lb.at[pl.ds(pl.multiple_of(q * 256, 256), 256)]
        return copy(LEFT, k, block, block, qpeer(k)[1])

    def right_copy(k):
        return copy(RIGHT, k, rbuf.at[z], rbuf.at[z], zpeer(k)[1])

    def rsum_copy(k, part):
        t, device = zpeer(k)
        half = pl.ds(part * 128, 128)
        return copy(RSUM + part, k, rss.at[t, half], rsr.at[k, half], device)

    def lsum_copy(k):
        t, device = qpeer(k)
        return copy(LSUM, k, lss.at[t], lsr.at[k], device)

    def group_copy(which, src, dst, device):
        return pltpu.make_async_remote_copy(
            src_ref=src, dst_ref=dst, send_sem=group_send.at[which], recv_sem=group_recv.at[which],
            device_id=device, device_id_type=MESH,
        )

    def scatter_plane(which, src, dst):
        @pl.loop(1, 32)
        def _(k):
            t, device = gpeer(k)
            group_copy(which, src.at[t], dst.at[k], device).start()

    def share_line(which, ref):
        for k in (4, 3, 5, 2, 6, 1, 7):
            group_copy(which, ref.at[z], ref.at[z], zpeer(k)[1]).start()

    def gather_plane(which, ref):
        @pl.loop(1, 32)
        def _(k):
            group_copy(which, ref.at[g], ref.at[g], gpeer(k)[1]).start()

    def group_wait(which, ref, sems):
        count = ref.shape[0] - 1
        pltpu.make_async_copy(ref.at[pl.ds(1, count)], ref.at[pl.ds(1, count)], sems.at[which]).wait()

    def start(make, count=8):
        for k in range(1, count):
            make(k).start()

    def arrived(make, count=8):
        for k in range(1, count):
            make(k).wait_recv()

    barrier = pltpu.get_barrier_semaphore()
    for k in range(1, 8):
        pl.semaphore_signal(barrier, inc=1, device_id=zpeer(k)[1], device_id_type=MESH)

    @pl.loop(1, 32)
    def _(k):
        pl.semaphore_signal(barrier, inc=1, device_id=gpeer(k)[1], device_id_type=MESH)

    for load in loads[:4]:
        load.wait()
    used = jnp.sum(seq_ref[...].astype(F32), axis=1, keepdims=True)
    res_j = res_ref[:, pl.ds(pl.multiple_of(col * 128, 128), 128)].astype(F32)
    res_j = jnp.broadcast_to(res_j, (128, 128)).T
    inv1[...] = 1.0 / jnp.maximum(used * res_j, 1.0)

    @pl.loop(0, 16, unroll=2)
    def _(i):
        res_i = res_s[row * 32 + core * 16 + i].astype(F32)
        scaled = pair_ref[i].astype(F32) * (inv1[...] * res_i + (1.0 - res_i))
        for t in range(8):
            piece = jnp.concatenate([scaled[t * 8 : t * 8 + 8], scaled[64 + t * 8 : 72 + t * 8]], axis=0)
            ps[t, i] = piece.astype(BF16)

    pl.semaphore_wait(barrier, 38)
    start(pair_copy)
    own_pair = pltpu.make_async_copy(ps.at[q], scb.at[core, col, h], local_sems.at[3])
    own_pair.start()

    for load in loads[4:11]:
        load.wait()
    pick = lax.broadcasted_iota(jnp.int32, (64, 32), 0) - lax.broadcasted_iota(jnp.int32, (64, 32), 1)
    first, second = (pick == 0).astype(F32), (pick == 32).astype(F32)
    wt[0:32, :] = wl_ref[...]
    wt[32:64, :] = wr_ref[...]
    exact = dict(precision=lax.Precision.HIGHEST)
    bias[...] = dot_nt(first, jnp.broadcast_to(lb_ref[...], (128, 32)), **exact) + dot_nt(
        second, jnp.broadcast_to(rb_ref[...], (128, 32)), **exact
    )
    for e in range(2):
        xf[e] = x_ref[:, e * 128 : e * 128 + 128].astype(F32)
    seq_row = seq_ref[:, pl.ds(pl.multiple_of(depth * 128, 128), 128)].astype(F32)
    own_first = (row * 4 + col) * 8

    @pl.loop(0, 8, unroll=4)
    def _(r):
        values = jnp.concatenate([xf[e, pl.ds(r, 128, stride=8), :] for e in range(2)], axis=1)
        centred = values - jnp.mean(values, axis=1, keepdims=True)
        inv_std = lax.rsqrt(jnp.mean(centred * centred, axis=1, keepdims=True) + 1e-05)
        units = centred * inv_std
        normed = (units * gain_ref[...] + shift_ref[...]).astype(BF16)
        unit[r] = units
        norm[r] = normed
        istd[r] = jnp.broadcast_to(inv_std, (128, 128))
        mask = seq_row * res_s[own_first + r].astype(F32)
        both = (dot_nt(wt[...], normed) + bias[...]) * mask
        lb[pl.ds(pl.multiple_of(q * 256 + r * 32, 32), 32), :] = both[:32].astype(BF16)
        rf[pl.ds(r, 32, stride=8), :] = both[32:]

    rbuf[z] = rf[...].astype(BF16)
    start(left_copy)
    for k in (4, 3, 5, 2, 6, 1, 7):
        right_copy(k).start()

    loads[11].wait()
    wf[...] = ow_ref[...].astype(F32)
    for d in range(32):
        wp[d // 2 * 32 : d // 2 * 32 + 32, d % 2 * 128 : d % 2 * 128 + 128] = wf[pl.ds(d, 32, stride=32), :].astype(BF16)

    @pl.loop(0, 64)
    def _(i):
        bd[i] = jnp.zeros((128, 256), BF16)

    own_pair.wait()
    other_copy(0).start()
    for k in range(1, 8):
        pair_copy(k).wait_recv()
        other_copy(k).start()

    def outer_grads(side):
        @pl.loop(0, 16, unroll=8)
        def _(t):
            upper, at = lax.div(t, 8), lax.rem(t, 8) * 2
            i = upper * 32 + side * 16 + at
            for e in range(2):
                block = jnp.concatenate([scb[side, y, upper, at + e] for y in range(4)], axis=0)
                bd[i + e, :64, :128] = block
                bd[i + e, 64:, 128:] = block
            grads = dot_nt(wp[...], bd[pl.ds(i, 2)].reshape(256, 256)).astype(BF16)
            for e in range(2):
                rows = pl.ds(pl.multiple_of((i + e) * 32, 32), 32)
                for p in range(16):
                    og[rows, p * 128 : p * 128 + 128] = grads[p * 32 : p * 32 + 32, e * 128 : e * 128 + 128]

    outer_grads(core)
    for k in range(8):
        other_copy(k).wait_recv()
    outer_grads(1 - core)

    arrived(left_copy)
    for t in range(16):
        block = lb[t * 128 : t * 128 + 128, :].astype(F32)
        lt[:, t * 128 : t * 128 + 128] = block.T.astype(BF16)

    def right_sums(part):
        sums = dot(lt[...], og[:, part * 1024 : part * 1024 + 1024])
        for p in range(8):
            turned = sums[:, p * 128 : p * 128 + 128].T
            at = part * 128 + p * 16
            for t in range(8):
                piece = jnp.concatenate([turned[t * 8 : t * 8 + 8], turned[64 + t * 8 : 72 + t * 8]], axis=0)
                rss[t, at : at + 16, :] = piece.astype(BF16)

    for part in range(2):
        right_sums(part)
        for k in (4, 3, 5, 2, 6, 1, 7):
            rsum_copy(k, part).start()

    arrived(right_copy)

    @pl.loop(0, 16, unroll=4)
    def _(p):
        blocks = [rbuf[t, pl.ds(pl.multiple_of(p * 16, 16), 16), :].astype(F32) for t in range(8)]
        rows = [block[:8] for block in blocks] + [block[8:] for block in blocks]
        rt[pl.ds(pl.multiple_of(p * 128, 128), 128), :] = jnp.concatenate(rows, axis=0).astype(BF16)

    def left_sum(t):
        at = pl.ds(pl.multiple_of(t * 256, 256), 256)
        lss[t] = dot(og[at, :], rt[...]).astype(BF16)

    def send_left(k):
        left_sum(lax.rem(q + k, 8))
        lsum_copy(k).start()

    @pl.loop(1, 8, unroll=7)
    def _(k):
        send_left(k)

    left_sum(q)

    @pl.loop(0, 8, unroll=4)
    def _(n):
        at = pl.ds(pl.multiple_of(n * 256, 256), 256)
        for m in range(4):
            product = dot_nt(lb[m * 512 : m * 512 + 512, :], rt[at, :])
            outer[m * 512 : m * 512 + 512, at] = product.astype(BF16)

    for t in range(2):
        blocks = [outer[(32 * t + e) * 32 : (32 * t + e) * 32 + 32, :] for e in range(32)]
        rows = [
            jnp.concatenate([block[:, p * 128 : p * 128 + 128] for block in blocks], axis=1) for p in range(16)
        ]
        part = dot(jnp.concatenate(rows, axis=0), bd[32 * t : 32 * t + 32].reshape(4096, 256))
        wga[...] = part if t == 0 else wga[...] + part

    for t in range(32):
        w1s[t] = wga[t * 16 : t * 16 + 16, :].astype(BF16)
    scatter_plane(W1, w1s, w1r)

    arrived(lsum_copy)
    total = lss[q].astype(F32)
    for k in range(1, 8):
        total = total + lsr[k].astype(F32)
    lsf[...] = total
    total = rss[z].astype(F32)
    for k in range(1, 8):
        rsum_copy(k, 0).wait_recv()
        rsum_copy(k, 1).wait_recv()
        total = total + rsr[k].astype(F32)
    rf[...] = total

    wgt[...] = jnp.zeros_like(wgt)
    extra[...] = jnp.zeros_like(extra)

    @pl.loop(0, 8, unroll=4)
    def _(r):
        mask = seq_row * res_s[own_first + r].astype(F32)
        sides = [lsf[pl.ds(pl.multiple_of(r * 32, 32), 32), :], rf[pl.ds(r, 32, stride=8), :]]
        pre = (jnp.concatenate(sides, axis=0) * mask).astype(BF16)
        grad = lax.dot_general(pre, wt[...], TN, preferred_element_type=F32)
        ngrad[r] = grad
        wgt[...] += dot(pre, norm[r])
        extra[0:1, :] += jnp.sum(grad * unit[r], axis=0, keepdims=True)
        extra[1:2, :] += jnp.sum(grad, axis=0, keepdims=True)
        extra[2:3, 0:64] += dot_nt(jnp.ones((8, 128), BF16), pre)[0:1]

    upper = lax.broadcasted_iota(jnp.int32, (8, 128), 0) < 4
    for t in range(16):
        tile = wgt[t // 2 * 8 : t // 2 * 8 + 8, t % 2 * 128 : t % 2 * 128 + 128]
        s1s[2 * t] = jnp.where(upper, tile, 0.0)
        s1s[2 * t + 1] = jnp.where(upper, 0.0, tile)
    s1s[0, 4:5, :] = extra[0:1, :128]
    s1s[1, 0:1, :] = extra[0:1, 128:]
    s1s[2, 4:5, :] = extra[1:2, :128]
    s1s[3, 0:1, :] = extra[1:2, 128:]
    s1s[4, 4:5, :] = extra[2:3, :128]
    scatter_plane(S1, s1s, s1r)

    def input_grad(r):
        units = unit[r]
        weighted = ngrad[r] * gain_ref[...]
        mean = jnp.mean(weighted, axis=1, keepdims=True)
        along = jnp.mean(weighted * units, axis=1, keepdims=True)
        scale = jnp.concatenate([istd[r], istd[r]], axis=1)
        result = scale * (weighted - mean - units * along)
        for e in range(2):
            xf[e, pl.ds(r, 128, stride=8), :] = result[:, e * 128 : e * 128 + 128]

    def summed(ref, count, first):
        total = first
        for k in range(1, count):
            total = total + ref[k].astype(F32)
        return total

    @pl.loop(0, 4, unroll=4)
    def _(r):
        input_grad(r)

    group_wait(W1, w1r, group_recv)
    w2[z] = summed(w1r, 32, wga[pl.ds(pl.multiple_of(g * 16, 16), 16), :]).astype(BF16)
    share_line(W2, w2)
    group_wait(S1, s1r, group_recv)
    s2[z] = summed(s1r, 32, s1s[g])
    share_line(S2, s2)

    @pl.loop(4, 8, unroll=4)
    def _(r):
        input_grad(r)

    for e in range(2):
        ag_ref[:, e * 128 : e * 128 + 128] = xf[e].astype(BF16)
    store = pltpu.make_async_copy(ag_ref, ag_any, local_sems.at[4])
    store.start()

    group_wait(W2, w2, group_recv)
    w3[g] = summed(w2, 8, w2[0].astype(F32)).astype(BF16)
    gather_plane(W3, w3)
    group_wait(S2, s2, group_recv)
    s3[g] = summed(s2, 8, s2[0])
    gather_plane(S3, s3)

    for make in (pair_copy, left_copy, lsum_copy):
        for k in range(1, 8):
            make(k).wait_send()
    for n in range(8):
        other_copy(n).wait_send()
    for k in range(1, 8):
        right_copy(k).wait_send()
    for k in range(1, 8):
        rsum_copy(k, 0).wait_send()
        rsum_copy(k, 1).wait_send()
    for which, ref in ((W1, w1s), (W2, w2), (W3, w3), (S1, s1s), (S2, s2), (S3, s3)):
        group_wait(which, ref, group_send)

    group_wait(W3, w3, group_recv)
    store_wg = pltpu.make_async_copy(w3, wg_any, local_sems.at[0])
    store_wg.start()
    group_wait(S3, s3, group_recv)
    store_sf = pltpu.make_async_copy(s3, sf_any, local_sems.at[1])
    store_sf.start()
    store.wait()
    store_wg.wait()
    store_sf.wait()


def last_kernel(
    ag_any, sf_any, wg_any, ag_out, lw_out, lb_out, rw_out, rb_out, gain_out, shift_out, ow_out,
    sf, wg, ag, lw, lb, rw, rb, gain, shift, ow, in_sems, out_sems,
):
    def load(n, src, dst):
        return pltpu.make_async_copy(src, dst, in_sems.at[n])

    def store(n, src, dst):
        return pltpu.make_async_copy(src, dst, out_sems.at[n])

    rows = [pl.ds(n * 256, 256) for n in range(4)]
    loads = [load(0, wg_any, wg), load(1, sf_any, sf)] + [
        load(2 + n, ag_any.at[part], ag.at[part]) for n, part in enumerate(rows)
    ]
    for move in loads:
        move.start()
    stores = []

    def send(src, dst):
        stores.append(store(len(stores), src, dst))
        stores[-1].start()

    loads[0].wait()
    for half in range(2):
        for d in range(32):
            tile = wg[d // 2 * 2 + half, :, d % 2 * 128 : d % 2 * 128 + 128]
            ow[pl.ds(half * 512 + d, 16, stride=32), :] = tile.astype(F32)
        send(ow.at[pl.ds(half * 512, 512)], ow_out.at[pl.ds(half * 512, 512)])
    loads[1].wait()
    upper = lax.broadcasted_iota(jnp.int32, (8, 128), 0) < 4
    for t in range(16):
        tile = jnp.where(upper, sf[2 * t], sf[2 * t + 1])
        side, row, lane = (lw, rw)[t // 8], t % 8 // 2 * 8, t % 2 * 128
        side[row : row + 8, lane : lane + 128] = tile
    gain[:, :128] = sf[0, 4:5, :]
    gain[:, 128:] = sf[1, 0:1, :]
    shift[:, :128] = sf[2, 4:5, :]
    shift[:, 128:] = sf[3, 0:1, :]
    lb[...] = sf[4, 4:5, 0:32]
    rb[...] = sf[4, 4:5, 32:64]
    for src, dst in ((lw, lw_out), (rw, rw_out), (lb, lb_out), (rb, rb_out), (gain, gain_out), (shift, shift_out)):
        send(src, dst)
    for n, part in enumerate(rows):
        loads[2 + n].wait()
        send(ag.at[part], ag_out.at[part])
    for move in stores:
        move.wait()


def body(
    alignment, seq_mask, residue_mask, layer_norm_gain, layer_norm_bias, left_projection_weight, left_bias,
    right_projection_weight, right_bias, out_weight, pair_grad,
):
    hbm = pl.BlockSpec(memory_space=pl.ANY)
    v = pltpu.VMEM
    shape = jax.ShapeDtypeStruct
    scratch = [
        v((16, 128, 128), BF16),
        v((1024, 256), BF16),
        v((1024, 128), BF16),
        v((1024, 256), BF16),
        v((1, 512), jnp.int32),
        v((1, 512), jnp.int32),
        pltpu.SMEM((512,), jnp.int32),
        v((1, 256), F32),
        v((1, 256), F32),
        v((32, 256), BF16),
        v((1, 32), F32),
        v((32, 256), BF16),
        v((1, 32), F32),
        v((128, 128), F32),
        v((2, 1024, 128), F32),
        v((8, 128, 256), F32),
        v((8, 128, 256), BF16),
        v((8, 128, 128), F32),
        v((8, 128, 256), F32),
        v((64, 256), BF16),
        v((64, 128), F32),
        v((1024, 128), F32),
        v((512, 256), BF16),
        v((8, 16, 16, 128), BF16),
        v((2, 4, 2, 16, 16, 128), BF16),
        v((64, 128, 256), BF16),
        v((2048, 2048), BF16),
        v((2048, 2048), BF16),
        v((2048, 128), BF16),
        v((128, 2048), BF16),
        v((256, 128), F32),
        v((8, 256, 128), BF16),
        v((2048, 128), BF16),
        v((8, 256, 128), BF16),
        v((8, 256, 128), BF16),
        v((8, 256, 128), BF16),
        v((8, 256, 128), BF16),
        v((256, 128), F32),
        v((512, 256), F32),
        v((32, 16, 256), BF16),
        v((32, 16, 256), BF16),
        v((8, 16, 256), BF16),
        v((32, 16, 256), BF16),
        v((64, 256), F32),
        v((8, 256), F32),
        v((32, 8, 128), F32),
        v((32, 8, 128), F32),
        v((8, 8, 128), F32),
        v((32, 8, 128), F32),
        pltpu.SemaphoreType.DMA((7, 8)),
        pltpu.SemaphoreType.DMA((7, 8)),
        pltpu.SemaphoreType.DMA((6,)),
        pltpu.SemaphoreType.DMA((6,)),
        pltpu.SemaphoreType.DMA((5,)),
        pltpu.SemaphoreType.DMA((12,)),
    ]
    ag, sf, wg = pl.pallas_call(
        main_kernel,
        out_shape=(shape((1024, 256), BF16), shape((32, 8, 128), F32), shape((32, 16, 256), BF16)),
        in_specs=[hbm] * 12,
        out_specs=(hbm,) * 3,
        scratch_shapes=scratch,
        compiler_params=pltpu.CompilerParams(
            collective_id=0, has_side_effects=True, vmem_limit_bytes=58 * 1024 * 1024
        ),
        name="pair_backward",
    )(
        alignment.reshape(1024, 256), seq_mask.reshape(1, 512), residue_mask.reshape(1, 512), residue_mask,
        layer_norm_gain.reshape(1, 256), layer_norm_bias.reshape(1, 256), left_projection_weight.T,
        left_bias.reshape(1, 32), right_projection_weight.T, right_bias.reshape(1, 32), out_weight, pair_grad,
    )
    ag, lw, lbg, rw, rbg, gain, shift, ow = pl.pallas_call(
        last_kernel,
        out_shape=(
            shape((1024, 256), BF16), shape((32, 256), F32), shape((1, 32), F32), shape((32, 256), F32),
            shape((1, 32), F32), shape((1, 256), F32), shape((1, 256), F32), shape((1024, 128), F32),
        ),
        in_specs=[pl.BlockSpec(memory_space=pl.ANY)] * 3,
        out_specs=(hbm,) * 8,
        scratch_shapes=[
            v((32, 8, 128), F32), v((32, 16, 256), BF16), v((1024, 256), BF16), v((32, 256), F32), v((1, 32), F32),
            v((32, 256), F32), v((1, 32), F32), v((1, 256), F32), v((1, 256), F32), v((1024, 128), F32),
            pltpu.SemaphoreType.DMA((6,)), pltpu.SemaphoreType.DMA((12,)),
        ],
        compiler_params=pltpu.CompilerParams(vmem_limit_bytes=58 * 1024 * 1024),
        name="lay_out",
    )(ag, sf, wg)
    return (
        ag.reshape(128, 8, 256), lw.T, lbg.reshape(32), rw.T, rbg.reshape(32), gain.reshape(256), shift.reshape(256), ow,
    )


def solution(mesh):
    placed = (P("depth", ("row", "col"), None),) + (P(),) * 9 + (P("row", "col", None),)
    return jax.shard_map(
        body,
        mesh=mesh,
        in_specs=placed,
        out_specs=(P("depth", ("row", "col"), None),) + (P(),) * 7,
        check_vma=False,
    )
```

```python
import jax
import jax.numpy as jnp
from jax import lax
from jax.experimental import pallas as pl
from jax.experimental.pallas import tpu as pltpu
from jax.sharding import PartitionSpec as P

F32, BF16 = jnp.float32, jnp.bfloat16
MESH = pl.DeviceIdType.MESH
NT = (((1,), (1,)), ((), ()))
TN = (((0,), (0,)), ((), ()))
PAIR, OTHER, LEFT, RIGHT, RSUM, RSUM2, LSUM = range(7)
W1, W2, W3, S1, S2, S3 = range(6)


def dot(a, b):
    return jnp.dot(a, b, preferred_element_type=F32)


def dot_nt(a, b, **kw):
    return lax.dot_general(a, b, NT, preferred_element_type=F32, **kw)


def main_kernel(
    x_any, seq_any, res_any, res_flat, gain_any, shift_any, wl_any, lb_any, wr_any, rb_any, ow_any, pair_any,
    ag_any, sf_any, wg_any,
    pair_ref, x_ref, ow_ref, ag_ref,
    seq_ref, res_ref, res_s, gain_ref, shift_ref, wl_ref, lb_ref, wr_ref, rb_ref, inv1, xf, unit, norm, istd, ngrad, wt, bias, wf, wp, ps, scb, bd, og, outer, lb, lt, rf, rbuf, rt,
    rss, rsr, lss, lsr, lsf, wga, w1s, w1r, w2, w3, wgt, extra, s1s, s1r, s2, s3,
    send_sem, recv_sem, group_send, group_recv, local_sems, load_sems,
):
    depth, row, col = lax.axis_index("depth"), lax.axis_index("row"), lax.axis_index("col")
    z, h = lax.div(row, 2), lax.rem(row, 2)
    q = h * 4 + col
    core = lax.rem(depth, 2)

    moves = (
        (pair_any.at[pl.ds(core * 16, 16)], pair_ref), (seq_any, seq_ref), (res_any, res_ref), (res_flat, res_s),
        (x_any, x_ref), (gain_any, gain_ref), (shift_any, shift_ref), (wl_any, wl_ref), (lb_any, lb_ref),
        (wr_any, wr_ref), (rb_any, rb_ref), (ow_any, ow_ref),
    )
    loads = [pltpu.make_async_copy(src, dst, load_sems.at[n]) for n, (src, dst) in enumerate(moves)]
    for load in loads:
        load.start()

    def zpeer(k):
        t = lax.rem(z + k, 8)
        return t, (depth, t * 2 + h, col)

    def qpeer(k):
        t = lax.rem(q + k, 8)
        return t, (depth, z * 2 + lax.div(t, 4), lax.rem(t, 4))

    g = depth * 8 + q

    def gpeer(k):
        t = lax.rem(g + k, 32)
        u = lax.rem(t, 8)
        return t, (lax.div(t, 8), z * 2 + lax.div(u, 4), lax.rem(u, 4))

    def copy(which, k, src, dst, device):
        return pltpu.make_async_remote_copy(
            src_ref=src, dst_ref=dst, send_sem=send_sem.at[which, k], recv_sem=recv_sem.at[which, k],
            device_id=device, device_id_type=MESH,
        )

    def pair_copy(k):
        t, device = qpeer(k)
        return copy(PAIR, k, ps.at[t], scb.at[core, col, h], device)

    def other_copy(k):
        t = lax.rem(q + 8 - k, 8)
        block = scb.at[core, lax.rem(t, 4), lax.div(t, 4)]
        return copy(OTHER, k, block, block, (depth + 1 - 2 * core, row, col))

    def left_copy(k):
        block = lb.at[pl.ds(pl.multiple_of(q * 256, 256), 256)]
        return copy(LEFT, k, block, block, qpeer(k)[1])

    def right_copy(k):
        return copy(RIGHT, k, rbuf.at[z], rbuf.at[z], zpeer(k)[1])

    def rsum_copy(k, part):
        t, device = zpeer(k)
        half = pl.ds(part * 128, 128)
        return copy(RSUM + part, k, rss.at[t, half], rsr.at[k, half], device)

    def lsum_copy(k):
        t, device = qpeer(k)
        return copy(LSUM, k, lss.at[t], lsr.at[k], device)

    def group_copy(which, src, dst, device):
        return pltpu.make_async_remote_copy(
            src_ref=src, dst_ref=dst, send_sem=group_send.at[which], recv_sem=group_recv.at[which],
            device_id=device, device_id_type=MESH,
        )

    def scatter_plane(which, src, dst):
        @pl.loop(1, 32)
        def _(k):
            t, device = gpeer(k)
            group_copy(which, src.at[t], dst.at[k], device).start()

    def share_line(which, ref):
        for k in (4, 3, 5, 2, 6, 1, 7):
            group_copy(which, ref.at[z], ref.at[z], zpeer(k)[1]).start()

    def gather_plane(which, ref):
        @pl.loop(1, 32)
        def _(k):
            group_copy(which, ref.at[g], ref.at[g], gpeer(k)[1]).start()

    def group_wait(which, ref, sems):
        count = ref.shape[0] - 1
        pltpu.make_async_copy(ref.at[pl.ds(1, count)], ref.at[pl.ds(1, count)], sems.at[which]).wait()

    def start(make, count=8):
        for k in range(1, count):
            make(k).start()

    def arrived(make, count=8):
        for k in range(1, count):
            make(k).wait_recv()

    barrier = pltpu.get_barrier_semaphore()
    for k in range(1, 8):
        pl.semaphore_signal(barrier, inc=1, device_id=zpeer(k)[1], device_id_type=MESH)

    @pl.loop(1, 32)
    def _(k):
        pl.semaphore_signal(barrier, inc=1, device_id=gpeer(k)[1], device_id_type=MESH)

    for load in loads[:4]:
        load.wait()
    used = jnp.sum(seq_ref[...].astype(F32), axis=1, keepdims=True)
    res_j = res_ref[:, pl.ds(pl.multiple_of(col * 128, 128), 128)].astype(F32)
    res_j = jnp.broadcast_to(res_j, (128, 128)).T
    inv1[...] = 1.0 / jnp.maximum(used * res_j, 1.0)

    @pl.loop(0, 16, unroll=2)
    def _(i):
        res_i = res_s[row * 32 + core * 16 + i].astype(F32)
        scaled = pair_ref[i].astype(F32) * (inv1[...] * res_i + (1.0 - res_i))
        for t in range(8):
            piece = jnp.concatenate([scaled[t * 8 : t * 8 + 8], scaled[64 + t * 8 : 72 + t * 8]], axis=0)
            ps[t, i] = piece.astype(BF16)

    pl.semaphore_wait(barrier, 38)
    start(pair_copy)
    own_pair = pltpu.make_async_copy(ps.at[q], scb.at[core, col, h], local_sems.at[3])
    own_pair.start()

    for load in loads[4:11]:
        load.wait()
    pick = lax.broadcasted_iota(jnp.int32, (64, 32), 0) - lax.broadcasted_iota(jnp.int32, (64, 32), 1)
    first, second = (pick == 0).astype(F32), (pick == 32).astype(F32)
    wt[0:32, :] = wl_ref[...]
    wt[32:64, :] = wr_ref[...]
    exact = dict(precision=lax.Precision.HIGHEST)
    bias[...] = dot_nt(first, jnp.broadcast_to(lb_ref[...], (128, 32)), **exact) + dot_nt(
        second, jnp.broadcast_to(rb_ref[...], (128, 32)), **exact
    )
    for e in range(2):
        xf[e] = x_ref[:, e * 128 : e * 128 + 128].astype(F32)
    seq_row = seq_ref[:, pl.ds(pl.multiple_of(depth * 128, 128), 128)].astype(F32)
    own_first = (row * 4 + col) * 8

    @pl.loop(0, 8, unroll=4)
    def _(r):
        values = jnp.concatenate([xf[e, pl.ds(r, 128, stride=8), :] for e in range(2)], axis=1)
        centred = values - jnp.mean(values, axis=1, keepdims=True)
        inv_std = lax.rsqrt(jnp.mean(centred * centred, axis=1, keepdims=True) + 1e-05)
        units = centred * inv_std
        normed = (units * gain_ref[...] + shift_ref[...]).astype(BF16)
        unit[r] = units
        norm[r] = normed
        istd[r] = jnp.broadcast_to(inv_std, (128, 128))
        mask = seq_row * res_s[own_first + r].astype(F32)
        both = (dot_nt(wt[...], normed) + bias[...]) * mask
        lb[pl.ds(pl.multiple_of(q * 256 + r * 32, 32), 32), :] = both[:32].astype(BF16)
        rf[pl.ds(r, 32, stride=8), :] = both[32:]

    rbuf[z] = rf[...].astype(BF16)
    start(left_copy)
    for k in (4, 3, 5, 2, 6, 1, 7):
        right_copy(k).start()

    loads[11].wait()
    wf[...] = ow_ref[...].astype(F32)
    for d in range(32):
        wp[d // 2 * 32 : d // 2 * 32 + 32, d % 2 * 128 : d % 2 * 128 + 128] = wf[pl.ds(d, 32, stride=32), :].astype(BF16)

    @pl.loop(0, 64)
    def _(i):
        bd[i] = jnp.zeros((128, 256), BF16)

    own_pair.wait()
    other_copy(0).start()
    for k in range(1, 8):
        pair_copy(k).wait_recv()
        other_copy(k).start()

    def outer_grads(side):
        @pl.loop(0, 16, unroll=8)
        def _(t):
            upper, at = lax.div(t, 8), lax.rem(t, 8) * 2
            i = upper * 32 + side * 16 + at
            for e in range(2):
                block = jnp.concatenate([scb[side, y, upper, at + e] for y in range(4)], axis=0)
                bd[i + e, :64, :128] = block
                bd[i + e, 64:, 128:] = block
            grads = dot_nt(wp[...], bd[pl.ds(i, 2)].reshape(256, 256)).astype(BF16)
            for e in range(2):
                rows = pl.ds(pl.multiple_of((i + e) * 32, 32), 32)
                for p in range(16):
                    og[rows, p * 128 : p * 128 + 128] = grads[p * 32 : p * 32 + 32, e * 128 : e * 128 + 128]

    outer_grads(core)
    for k in range(8):
        other_copy(k).wait_recv()
    outer_grads(1 - core)

    arrived(right_copy)

    @pl.loop(0, 16, unroll=4)
    def _(p):
        blocks = [rbuf[t, pl.ds(pl.multiple_of(p * 16, 16), 16), :].astype(F32) for t in range(8)]
        rows = [block[:8] for block in blocks] + [block[8:] for block in blocks]
        rt[pl.ds(pl.multiple_of(p * 128, 128), 128), :] = jnp.concatenate(rows, axis=0).astype(BF16)

    arrived(left_copy)
    for t in range(16):
        block = lb[t * 128 : t * 128 + 128, :].astype(F32)
        lt[:, t * 128 : t * 128 + 128] = block.T.astype(BF16)

    def right_sums(part):
        sums = dot(lt[...], og[:, part * 1024 : part * 1024 + 1024])
        for p in range(8):
            turned = sums[:, p * 128 : p * 128 + 128].T
            at = part * 128 + p * 16
            for t in range(8):
                piece = jnp.concatenate([turned[t * 8 : t * 8 + 8], turned[64 + t * 8 : 72 + t * 8]], axis=0)
                rss[t, at : at + 16, :] = piece.astype(BF16)

    for part in range(2):
        right_sums(part)
        for k in (4, 3, 5, 2, 6, 1, 7):
            rsum_copy(k, part).start()

    def left_sum(t):
        at = pl.ds(pl.multiple_of(t * 256, 256), 256)
        lss[t] = dot(og[at, :], rt[...]).astype(BF16)

    def send_left(k):
        left_sum(lax.rem(q + k, 8))
        lsum_copy(k).start()

    @pl.loop(1, 8, unroll=7)
    def _(k):
        send_left(k)


    @pl.loop(0, 8, unroll=4)
    def _(n):
        at = pl.ds(pl.multiple_of(n * 256, 256), 256)
        for m in range(4):
            product = dot_nt(lb[m * 512 : m * 512 + 512, :], rt[at, :])
            outer[m * 512 : m * 512 + 512, at] = product.astype(BF16)

    for t in range(2):
        blocks = [outer[(32 * t + e) * 32 : (32 * t + e) * 32 + 32, :] for e in range(32)]
        rows = [
            jnp.concatenate([block[:, p * 128 : p * 128 + 128] for block in blocks], axis=1) for p in range(16)
        ]
        part = dot(jnp.concatenate(rows, axis=0), bd[32 * t : 32 * t + 32].reshape(4096, 256))
        wga[...] = part if t == 0 else wga[...] + part

    for t in range(32):
        w1s[t] = wga[t * 16 : t * 16 + 16, :].astype(BF16)
    scatter_plane(W1, w1s, w1r)
    left_sum(q)

    arrived(lsum_copy)
    total = lss[q].astype(F32)
    for k in range(1, 8):
        total = total + lsr[k].astype(F32)
    lsf[...] = total
    total = rss[z].astype(F32)
    for k in range(1, 8):
        rsum_copy(k, 0).wait_recv()
        rsum_copy(k, 1).wait_recv()
        total = total + rsr[k].astype(F32)
    rf[...] = total

    wgt[...] = jnp.zeros_like(wgt)
    extra[...] = jnp.zeros_like(extra)

    @pl.loop(0, 8, unroll=4)
    def _(r):
        mask = seq_row * res_s[own_first + r].astype(F32)
        sides = [lsf[pl.ds(pl.multiple_of(r * 32, 32), 32), :], rf[pl.ds(r, 32, stride=8), :]]
        pre = (jnp.concatenate(sides, axis=0) * mask).astype(BF16)
        grad = lax.dot_general(pre, wt[...], TN, preferred_element_type=F32)
        ngrad[r] = grad
        wgt[...] += dot(pre, norm[r])
        extra[0:1, :] += jnp.sum(grad * unit[r], axis=0, keepdims=True)
        extra[1:2, :] += jnp.sum(grad, axis=0, keepdims=True)
        extra[2:3, 0:64] += dot_nt(jnp.ones((8, 128), BF16), pre)[0:1]

    upper = lax.broadcasted_iota(jnp.int32, (8, 128), 0) < 4
    for t in range(16):
        tile = wgt[t // 2 * 8 : t // 2 * 8 + 8, t % 2 * 128 : t % 2 * 128 + 128]
        s1s[2 * t] = jnp.where(upper, tile, 0.0)
        s1s[2 * t + 1] = jnp.where(upper, 0.0, tile)
    s1s[0, 4:5, :] = extra[0:1, :128]
    s1s[1, 0:1, :] = extra[0:1, 128:]
    s1s[2, 4:5, :] = extra[1:2, :128]
    s1s[3, 0:1, :] = extra[1:2, 128:]
    s1s[4, 4:5, :] = extra[2:3, :128]
    scatter_plane(S1, s1s, s1r)

    def input_grad(r):
        units = unit[r]
        weighted = ngrad[r] * gain_ref[...]
        mean = jnp.mean(weighted, axis=1, keepdims=True)
        along = jnp.mean(weighted * units, axis=1, keepdims=True)
        scale = jnp.concatenate([istd[r], istd[r]], axis=1)
        result = scale * (weighted - mean - units * along)
        for e in range(2):
            xf[e, pl.ds(r, 128, stride=8), :] = result[:, e * 128 : e * 128 + 128]

    def summed(ref, count, first):
        total = first
        for k in range(1, count):
            total = total + ref[k].astype(F32)
        return total

    @pl.loop(0, 4, unroll=4)
    def _(r):
        input_grad(r)

    group_wait(W1, w1r, group_recv)
    w2[z] = summed(w1r, 32, wga[pl.ds(pl.multiple_of(g * 16, 16), 16), :]).astype(BF16)
    share_line(W2, w2)
    group_wait(S1, s1r, group_recv)
    s2[z] = summed(s1r, 32, s1s[g])
    share_line(S2, s2)

    @pl.loop(4, 8, unroll=4)
    def _(r):
        input_grad(r)

    for e in range(2):
        ag_ref[:, e * 128 : e * 128 + 128] = xf[e].astype(BF16)
    store = pltpu.make_async_copy(ag_ref, ag_any, local_sems.at[4])
    store.start()

    group_wait(W2, w2, group_recv)
    w3[g] = summed(w2, 8, w2[0].astype(F32)).astype(BF16)
    gather_plane(W3, w3)
    group_wait(S2, s2, group_recv)
    s3[g] = summed(s2, 8, s2[0])
    gather_plane(S3, s3)

    for make in (pair_copy, left_copy, lsum_copy):
        for k in range(1, 8):
            make(k).wait_send()
    for n in range(8):
        other_copy(n).wait_send()
    for k in range(1, 8):
        right_copy(k).wait_send()
    for k in range(1, 8):
        rsum_copy(k, 0).wait_send()
        rsum_copy(k, 1).wait_send()
    for which, ref in ((W1, w1s), (W2, w2), (W3, w3), (S1, s1s), (S2, s2), (S3, s3)):
        group_wait(which, ref, group_send)

    group_wait(W3, w3, group_recv)
    store_wg = pltpu.make_async_copy(w3, wg_any, local_sems.at[0])
    store_wg.start()
    group_wait(S3, s3, group_recv)
    store_sf = pltpu.make_async_copy(s3, sf_any, local_sems.at[1])
    store_sf.start()
    store.wait()
    store_wg.wait()
    store_sf.wait()


def last_kernel(
    ag_any, sf_any, wg_any, ag_out, lw_out, lb_out, rw_out, rb_out, gain_out, shift_out, ow_out,
    sf, wg, ag, lw, lb, rw, rb, gain, shift, ow, in_sems, out_sems,
):
    def load(n, src, dst):
        return pltpu.make_async_copy(src, dst, in_sems.at[n])

    def store(n, src, dst):
        return pltpu.make_async_copy(src, dst, out_sems.at[n])

    rows = [pl.ds(n * 256, 256) for n in range(4)]
    loads = [load(0, wg_any, wg), load(1, sf_any, sf)] + [
        load(2 + n, ag_any.at[part], ag.at[part]) for n, part in enumerate(rows)
    ]
    for move in loads:
        move.start()
    stores = []

    def send(src, dst):
        stores.append(store(len(stores), src, dst))
        stores[-1].start()

    loads[0].wait()
    for half in range(2):
        for d in range(32):
            tile = wg[d // 2 * 2 + half, :, d % 2 * 128 : d % 2 * 128 + 128]
            ow[pl.ds(half * 512 + d, 16, stride=32), :] = tile.astype(F32)
        send(ow.at[pl.ds(half * 512, 512)], ow_out.at[pl.ds(half * 512, 512)])
    loads[1].wait()
    upper = lax.broadcasted_iota(jnp.int32, (8, 128), 0) < 4
    for t in range(16):
        tile = jnp.where(upper, sf[2 * t], sf[2 * t + 1])
        side, row, lane = (lw, rw)[t // 8], t % 8 // 2 * 8, t % 2 * 128
        side[row : row + 8, lane : lane + 128] = tile
    gain[:, :128] = sf[0, 4:5, :]
    gain[:, 128:] = sf[1, 0:1, :]
    shift[:, :128] = sf[2, 4:5, :]
    shift[:, 128:] = sf[3, 0:1, :]
    lb[...] = sf[4, 4:5, 0:32]
    rb[...] = sf[4, 4:5, 32:64]
    for src, dst in ((lw, lw_out), (rw, rw_out), (lb, lb_out), (rb, rb_out), (gain, gain_out), (shift, shift_out)):
        send(src, dst)
    for n, part in enumerate(rows):
        loads[2 + n].wait()
        send(ag.at[part], ag_out.at[part])
    for move in stores:
        move.wait()


def body(
    alignment, seq_mask, residue_mask, layer_norm_gain, layer_norm_bias, left_projection_weight, left_bias,
    right_projection_weight, right_bias, out_weight, pair_grad,
):
    hbm = pl.BlockSpec(memory_space=pl.ANY)
    v = pltpu.VMEM
    shape = jax.ShapeDtypeStruct
    scratch = [
        v((16, 128, 128), BF16),
        v((1024, 256), BF16),
        v((1024, 128), BF16),
        v((1024, 256), BF16),
        v((1, 512), jnp.int32),
        v((1, 512), jnp.int32),
        pltpu.SMEM((512,), jnp.int32),
        v((1, 256), F32),
        v((1, 256), F32),
        v((32, 256), BF16),
        v((1, 32), F32),
        v((32, 256), BF16),
        v((1, 32), F32),
        v((128, 128), F32),
        v((2, 1024, 128), F32),
        v((8, 128, 256), F32),
        v((8, 128, 256), BF16),
        v((8, 128, 128), F32),
        v((8, 128, 256), F32),
        v((64, 256), BF16),
        v((64, 128), F32),
        v((1024, 128), F32),
        v((512, 256), BF16),
        v((8, 16, 16, 128), BF16),
        v((2, 4, 2, 16, 16, 128), BF16),
        v((64, 128, 256), BF16),
        v((2048, 2048), BF16),
        v((2048, 2048), BF16),
        v((2048, 128), BF16),
        v((128, 2048), BF16),
        v((256, 128), F32),
        v((8, 256, 128), BF16),
        v((2048, 128), BF16),
        v((8, 256, 128), BF16),
        v((8, 256, 128), BF16),
        v((8, 256, 128), BF16),
        v((8, 256, 128), BF16),
        v((256, 128), F32),
        v((512, 256), F32),
        v((32, 16, 256), BF16),
        v((32, 16, 256), BF16),
        v((8, 16, 256), BF16),
        v((32, 16, 256), BF16),
        v((64, 256), F32),
        v((8, 256), F32),
        v((32, 8, 128), F32),
        v((32, 8, 128), F32),
        v((8, 8, 128), F32),
        v((32, 8, 128), F32),
        pltpu.SemaphoreType.DMA((7, 8)),
        pltpu.SemaphoreType.DMA((7, 8)),
        pltpu.SemaphoreType.DMA((6,)),
        pltpu.SemaphoreType.DMA((6,)),
        pltpu.SemaphoreType.DMA((5,)),
        pltpu.SemaphoreType.DMA((12,)),
    ]
    ag, sf, wg = pl.pallas_call(
        main_kernel,
        out_shape=(shape((1024, 256), BF16), shape((32, 8, 128), F32), shape((32, 16, 256), BF16)),
        in_specs=[hbm] * 12,
        out_specs=(hbm,) * 3,
        scratch_shapes=scratch,
        compiler_params=pltpu.CompilerParams(
            collective_id=0, has_side_effects=True, vmem_limit_bytes=58 * 1024 * 1024
        ),
        name="pair_backward",
    )(
        alignment.reshape(1024, 256), seq_mask.reshape(1, 512), residue_mask.reshape(1, 512), residue_mask,
        layer_norm_gain.reshape(1, 256), layer_norm_bias.reshape(1, 256), left_projection_weight.T,
        left_bias.reshape(1, 32), right_projection_weight.T, right_bias.reshape(1, 32), out_weight, pair_grad,
    )
    ag, lw, lbg, rw, rbg, gain, shift, ow = pl.pallas_call(
        last_kernel,
        out_shape=(
            shape((1024, 256), BF16), shape((32, 256), F32), shape((1, 32), F32), shape((32, 256), F32),
            shape((1, 32), F32), shape((1, 256), F32), shape((1, 256), F32), shape((1024, 128), F32),
        ),
        in_specs=[pl.BlockSpec(memory_space=pl.ANY)] * 3,
        out_specs=(hbm,) * 8,
        scratch_shapes=[
            v((32, 8, 128), F32), v((32, 16, 256), BF16), v((1024, 256), BF16), v((32, 256), F32), v((1, 32), F32),
            v((32, 256), F32), v((1, 32), F32), v((1, 256), F32), v((1, 256), F32), v((1024, 128), F32),
            pltpu.SemaphoreType.DMA((6,)), pltpu.SemaphoreType.DMA((12,)),
        ],
        compiler_params=pltpu.CompilerParams(vmem_limit_bytes=58 * 1024 * 1024),
        name="lay_out",
    )(ag, sf, wg)
    return (
        ag.reshape(128, 8, 256), lw.T, lbg.reshape(32), rw.T, rbg.reshape(32), gain.reshape(256), shift.reshape(256), ow,
    )


def solution(mesh):
    placed = (P("depth", ("row", "col"), None),) + (P(),) * 9 + (P("row", "col", None),)
    return jax.shard_map(
        body,
        mesh=mesh,
        in_specs=placed,
        out_specs=(P("depth", ("row", "col"), None),) + (P(),) * 7,
        check_vma=False,
    )
```
